128 devices in a mesh: island: 4 (over y_lo, core), mp: 32 (over z, x, y_hi).
Axes of the slice: x: 4, y: 4 (y_hi: 2, y_lo: 2; y = y_hi * 2 + y_lo), z: 4, core: 2. Of those that a mesh axis runs over, the one named last changes fastest.
Arguments:
- hidden: bfloat16 [4, 4096, 14336], P('island', None, 'mp'), may hold values from -6 to 6
- cotangent: bfloat16 [4, 4096, 4096], P('island', 'mp'), may hold values from -6 to 6
- local_weight: bfloat16 [4, 4096, 14336], P('island', None, 'mp'), may hold values from -6 to 6
- pending: bfloat16 [4, 4096, 14336], P('island', None, 'mp'), may hold values from -3 to 3
- global_weight: float32 [4096, 14336], P('island', 'mp'), may hold values from -6 to 6
- outer_momentum: float32 [4096, 14336], P('island', 'mp'), may hold values from -3 to 3
Outputs:
- hidden_grad: bfloat16 [4, 4096, 14336], P('island', None, 'mp')
- merged_weight: bfloat16 [4, 4096, 14336], P('island', None, 'mp')
- new_global: float32 [4096, 14336], P('island', 'mp')
- new_momentum: float32 [4096, 14336], P('island', 'mp')
The draws below stay inside these ranges and needn't reach their ends.
All inputs are finite; a program needn't handle non-finite values.
Results may differ from the reference program's by a relative error of at most 0.0065.
Values may be sent and summed in bfloat16 or wider, within the bound.
A program may use at most 128 MiB of HBM per device.

```python
import math
import jax
import jax.numpy as jnp
from jax import lax

D = 4096
FF = 14336
TOKENS = 4096
N_ISLAND = 4


def steps_of(rng, extent, cuts, smallest, largest):
    gain = 1.0
    for position, shards_of in cuts:
        steps = jax.random.uniform(jax.random.fold_in(jax.random.fold_in(rng, 6), position), (shards_of,), jnp.float32, smallest / len(cuts), largest / len(cuts))
        gain = gain * jnp.repeat(jnp.exp(steps), extent[position] // shards_of).reshape((-1,) + (1,) * (len(extent) - 1 - position))
    return gain


def noise(own_key, dims, deviation, limit, cuts=(), dtype=jnp.bfloat16):
    entries = jax.random.normal(own_key, dims, jnp.float32) * deviation
    if len(cuts) > 0:
        entries = steps_of(own_key, dims, cuts, -0.22, 0.18) * entries
    return jnp.clip(entries, min=-limit, max=limit).astype(dtype)


def setup_inputs(seed: int = 0) -> dict:
    key_of = jax.random.split(jax.random.key(seed), 7)
    return {
        "hidden": noise(key_of[0], (N_ISLAND, TOKENS, FF), 1.0, 6.0, ((0, 4), (2, 32))),
        "cotangent": noise(key_of[1], (N_ISLAND, TOKENS, D), 1.0, 6.0, ((0, 4), (1, 32))),
        "local_weight": noise(key_of[2], (N_ISLAND, D, FF), 1.0, 6.0, ((0, 4), (2, 32))),
        "pending": noise(key_of[3], (N_ISLAND, D, FF), 0.5, 3.0, ((0, 4), (2, 32))),
        "global_weight": noise(key_of[4], (D, FF), 1.0, 6.0, ((0, 4), (1, 32)), jnp.float32),
        "outer_momentum": noise(key_of[5], (D, FF), 0.5, 3.0, ((0, 4), (1, 32)), jnp.float32),
    }


inner_rate = 0.3
outer_rate = 0.7
decay_rate = 0.9
mix_weight = 0.5

def reference(hidden, cotangent, local_weight, pending, global_weight, outer_momentum):
    total_pending = jnp.zeros(global_weight.shape, jnp.float32)
    for island in range(N_ISLAND):
        total_pending = total_pending + pending[island].astype(jnp.float32)
    mean_pseudo = total_pending / N_ISLAND
    new_momentum = decay_rate * outer_momentum + mean_pseudo
    new_global = global_weight - outer_rate * (mean_pseudo + decay_rate * new_momentum)
    global_copy = lax.optimization_barrier(new_global.astype(jnp.bfloat16)).astype(jnp.float32)
    grad_list = []
    merged_list = []
    for island in range(N_ISLAND):
        activation = hidden[island]
        grads_out = cotangent[island]
        weight = local_weight[island]
        grad_block = jnp.dot(grads_out, weight, preferred_element_type=jnp.float32) * (1.0 / math.sqrt(D))
        grad_list.append(grad_block.astype(jnp.bfloat16))
        weight_grad = jnp.dot(grads_out.T, activation, preferred_element_type=jnp.float32) * (1.0 / math.sqrt(TOKENS))
        mixed = mix_weight * (weight.astype(jnp.float32) - inner_rate * weight_grad) + (1.0 - mix_weight) * global_copy
        merged_list.append(mixed.astype(jnp.bfloat16))
    return (jnp.stack(grad_list), jnp.stack(merged_list), new_global, new_momentum)
```

```python
import math

import jax
import jax.numpy as jnp
from jax import lax
from jax.experimental import pallas as pl
from jax.experimental.pallas import tpu as pltpu
from jax.sharding import PartitionSpec as P

D = 4096
TOKENS = 4096
FF_SHARE = 448
SHARD = 128

inner_rate = 0.3
outer_rate = 0.7
decay_rate = 0.9
mix_weight = 0.5
islands = 4

MESH = pl.DeviceIdType.MESH
MIB = 2**20

PIECES = (
    (0, 32, 0, True, 1),
    (32, 16, 0, True, -1),
    (48, 16, 0, False, -1),
    (64, 32, 1, True, 1),
    (96, 16, 1, True, -1),
    (112, 16, 1, False, -1),
)
LINKS = ((0, 1), (0, -1), (1, 1), (1, -1), (2, 1))
WRAP = (4, 4, 2)


def moved(offset, link):
    axis, step = LINKS[link]
    out = list(offset)
    out[axis] = (out[axis] + step) % WRAP[axis]
    return tuple(out)


def links_of(piece, offset):
    _, _, first, early, way = PIECES[piece]
    second = 1 - first
    found = []
    if offset[2] == 0 and (offset[first], offset[second]) == (0, 0) and early:
        found.append(4)
    if early or offset[2] == 0:
        for axis in (first, second):
            if axis == first and offset[second] != 0:
                continue
            turn = way if axis == first or offset[first] % 2 == 0 else -way
            for step in (1, -1):
                link = LINKS.index((axis, step))
                if offset[axis] == 0 or (offset[axis] == step % 4 and turn == step):
                    found.append(link)
    if offset[2] == 0 and not early:
        found.append(4)
    return found


def depth_of(piece, offset):
    best = 0.0
    for link in links_of(piece, offset):
        best = max(best, 1.0 + depth_of(piece, moved(offset, link)))
    return best


def plan():
    unit = 2.87 / 16
    latency = 2.0
    hg_time, wg_time = 2.2, 2.2
    heaps = [[] for _ in LINKS]
    free_at = [0.0] * len(LINKS)
    queued = [[] for _ in LINKS]
    arrivals = []
    steps = []
    have = {}
    now = 0.0
    sent_rows = [0] * len(LINKS)
    todo_hg, todo_wg = [], []
    islands_due = [(8.0, "reduce"), (34.0, "outer"), (62.0, "relay"), (76.0, "blend")]
    pieces = range(len(PIECES))

    def offer(item):
        for link in links_of(*item):
            heaps[link].append((-depth_of(item[0], moved(item[1], link)), now, item))

    def pump():
        for link in range(len(LINKS)):
            while True:
                queued[link] = [t for t in queued[link] if t > now]
                if len(queued[link]) >= 3 or not heaps[link]:
                    break
                heaps[link].sort()
                _, _, item = heaps[link].pop(0)
                rows = PIECES[item[0]][1]
                start = max(now, free_at[link])
                free_at[link] = start + unit * rows
                queued[link].append(free_at[link])
                sent_rows[link] += rows
                steps.append(("send", item, link))
                arrivals.append((free_at[link] + latency, (item[0], moved(item[1], link))))

    def land(item):
        have[item] = True
        offset = item[1]
        pair = offset[:2]
        if all((p, pair + (dy,)) in have for p in pieces for dy in (0, 1)):
            todo_hg.append(pair)
            todo_wg.append(pair)

    for p in pieces:
        item = (p, (0, 0, 0))
        have[item] = True
        offer(item)
    pump()
    total = len(PIECES) * 32
    first_wg = True
    while len(have) < total or todo_hg or todo_wg or islands_due:
        arrivals.sort()
        while arrivals and arrivals[0][0] <= now:
            _, item = arrivals.pop(0)
            steps.append(("wait", item))
            land(item)
            offer(item)
            now += 0.06
        pump()
        if islands_due and islands_due[0][0] <= now and not (islands_due[0][1] == "blend" and first_wg):
            steps.append(("task", islands_due.pop(0)[1]))
            now += 4.0
        elif todo_hg and len(todo_hg) >= len(todo_wg):
            steps.append(("task", "hg", todo_hg.pop(0)))
            now += hg_time
        elif todo_wg:
            steps.append(("task", "wg", todo_wg.pop(0), first_wg))
            first_wg = False
            now += wg_time
        else:
            times = [t for t, _ in arrivals[:1]] + [t for t, _ in islands_due[:1]]
            for q in queued:
                if len(q) >= 3:
                    times.append(min(q))
            times = [t for t in times if t > now]
            now = min(times) if times else now + 0.1
    last = max(i for i, s in enumerate(steps) if s[0] == "task" and s[1] == "wg")
    steps[last] = ("task", "end") + steps[last][2:3]
    return steps, sent_rows, now


def kernel(
    hidden, cotangent, local_weight, pending, global_weight, outer_momentum,
    hidden_grad, merged, new_global, new_momentum, fresh,
    c_buf, h_buf, w_buf, acc, hg_buf, p_buf, pc_buf, py_buf, g_buf, m_buf,
    send_sem, recv_sem, load_sem, hg_sem, out_sem, isl_send, isl_recv,
):
    island = lax.axis_index("island")
    mp = lax.axis_index("mp")
    z, x, yh = mp // 8, (mp // 2) % 4, mp % 2
    core, yl = island % 2, island // 2

    def mp_at(pz, px, py):
        return (lax.rem(pz, 4) * 4 + lax.rem(px, 4)) * 2 + lax.rem(py, 2)

    partner = [
        {"mp": mp_at(z + 1, x, yh)},
        {"mp": mp_at(z + 3, x, yh)},
        {"mp": mp_at(z, x + 1, yh)},
        {"mp": mp_at(z, x + 3, yh)},
        {"mp": mp_at(z, x, yh + 1)},
    ]
    other_core = {"island": yl * 2 + 1 - core}
    other_y = {"island": (1 - yl) * 2 + core}

    loads = [
        pltpu.make_async_copy(cotangent.at[0], c_buf.at[pl.ds(pl.multiple_of(mp * SHARD, SHARD), SHARD)], load_sem.at[0]),
        pltpu.make_async_copy(local_weight.at[0], w_buf, load_sem.at[1]),
        pltpu.make_async_copy(hidden.at[0], h_buf, load_sem.at[2]),
        pltpu.make_async_copy(global_weight, g_buf, load_sem.at[3]),
        pltpu.make_async_copy(outer_momentum, m_buf, load_sem.at[4]),
    ]

    def quarter(ref, index):
        return ref.at[pl.ds(pl.multiple_of(index * 1024, 1024), 1024)]

    mine, theirs = yl * 2 + core, (1 - yl) * 2 + core
    p_loads = [
        pltpu.make_async_copy(quarter(pending.at[0], theirs), p_buf.at[0], load_sem.at[5]),
        pltpu.make_async_copy(quarter(pending.at[0], mine), p_buf.at[1], load_sem.at[6]),
    ]
    for copy in loads + p_loads:
        copy.start()

    barrier = pltpu.get_barrier_semaphore()
    for device in partner + [other_core, other_y]:
        pl.semaphore_signal(barrier, inc=1, device_id=device, device_id_type=MESH)
    pl.semaphore_wait(barrier, len(partner) + 2)

    def rows_of(offset):
        dz, dx, dy = offset
        return mp_at(z + 4 - dz, x + 4 - dx, yh + dy) * SHARD

    def index_of(offset):
        return (offset[0] * 4 + offset[1]) * 2 + offset[2]

    def place(item):
        first, rows = PIECES[item[0]][:2]
        return c_buf.at[pl.ds(pl.multiple_of(rows_of(item[1]) + first, 16), rows)]

    def remote(src, dst, ssem, rsem, device):
        return pltpu.make_async_remote_copy(src, dst, ssem, rsem, device_id=device, device_id_type=MESH)

    def passing(item, link):
        dst = place(item)
        first, rows = PIECES[item[0]][:2]
        src = cotangent.at[0, pl.ds(first, rows)] if item[1] == (0, 0, 0) else dst
        return remote(src, dst, send_sem.at[link], recv_sem.at[index_of(moved(item[1], link)), item[0]], partner[link])

    def landed(item):
        dst = place(item)
        remote(dst, dst, send_sem.at[0], recv_sem.at[index_of(item[1]), item[0]], partner[0]).wait_recv()

    swap = [
        remote(quarter(pending.at[0], half * 2 + 1 - core), pc_buf.at[half], isl_send.at[half], isl_recv.at[half], other_core)
        for half in (0, 1)
    ]
    for copy in swap:
        copy.start()
    to_y = remote(p_buf.at[0], py_buf, isl_send.at[2], isl_recv.at[2], other_y)
    fresh_y = remote(p_buf.at[1], quarter(fresh, mine), isl_send.at[3], isl_recv.at[3], other_y)
    fresh_c = remote(p_buf.at[1], quarter(fresh, mine), isl_send.at[4], isl_recv.at[4], other_core)
    relay_c = remote(quarter(fresh, theirs), quarter(fresh, theirs), isl_send.at[5], isl_recv.at[5], other_core)
    ng_out = pltpu.make_async_copy(g_buf, new_global, out_sem.at[8])
    nm_out = pltpu.make_async_copy(m_buf, new_momentum, out_sem.at[9])

    backward_scale = 1.0 / math.sqrt(D)
    blend = -mix_weight * inner_rate / math.sqrt(TOKENS)
    tile = 256

    def reduce():
        for copy in p_loads:
            copy.wait()
        for copy in swap:
            copy.wait()

        def step(i, _):
            rows = pl.ds(pl.multiple_of(i * tile, tile), tile)
            p_buf[0, rows] = (p_buf[0, rows].astype(jnp.float32) + pc_buf[1 - yl, rows].astype(jnp.float32)).astype(jnp.bfloat16)
            return 0

        lax.fori_loop(0, 1024 // tile, step, 0)
        to_y.start()

    def outer():
        loads[3].wait()
        loads[4].wait()
        to_y.wait()

        def step(i, _):
            rows = pl.ds(pl.multiple_of(i * tile, tile), tile)
            mean = (
                p_buf[1, rows].astype(jnp.float32) + pc_buf[yl, rows].astype(jnp.float32) + py_buf[rows].astype(jnp.float32)
            ) / islands
            momentum = decay_rate * m_buf[rows] + mean
            weight = g_buf[rows] - outer_rate * (mean + decay_rate * momentum)
            m_buf[rows] = momentum
            g_buf[rows] = weight
            p_buf[1, rows] = weight.astype(jnp.bfloat16)
            return 0

        lax.fori_loop(0, 1024 // tile, step, 0)
        fresh_y.start()
        fresh_c.start()
        ng_out.start()
        nm_out.start()

    def relay():
        fresh_y.wait()
        relay_c.start()

    def add_base(source, index):
        def step(i, _):
            rows = pl.ds(pl.multiple_of(i * tile, tile), tile)
            full = pl.ds(pl.multiple_of(index * 1024 + i * tile, tile), tile)
            base = mix_weight * w_buf[full].astype(jnp.float32) + (1.0 - mix_weight) * p_buf[source, rows].astype(jnp.float32)
            acc[full] += base * (1.0 / blend)
            return 0

        lax.fori_loop(0, 1024 // tile, step, 0)

    def blend_all():
        fresh_c.wait()
        relay_c.wait()
        add_base(1, mine)
        for index in (theirs, yl * 2 + 1 - core, (1 - yl) * 2 + 1 - core):
            load = pltpu.make_async_copy(quarter(fresh, index), p_buf.at[0], load_sem.at[7])
            load.start()
            load.wait()
            add_base(0, index)

    def pair_rows(pair):
        return pl.multiple_of(mp_at(z + 4 - pair[0], x + 4 - pair[1], 0) * SHARD, 2 * SHARD)

    hg_copies = []

    def hg(pair):
        first = pair_rows(pair)
        rows = pl.ds(first, 2 * SHARD)
        slot = len(hg_copies) % 2
        if len(hg_copies) == 0:
            loads[0].wait()
            loads[1].wait()
        if len(hg_copies) >= 2:
            hg_copies[-2].wait()
        block = jnp.dot(c_buf[rows], w_buf[...], preferred_element_type=jnp.float32) * backward_scale
        hg_buf[slot] = block.astype(jnp.bfloat16)
        copy = pltpu.make_async_copy(hg_buf.at[slot], hidden_grad.at[0, rows], hg_sem.at[slot])
        copy.start()
        hg_copies.append(copy)

    width = 512

    def product(first, i):
        columns = pl.ds(pl.multiple_of(i * width, width), width)
        rows = pl.ds(first, 2 * SHARD)
        return columns, lax.dot_general(
            c_buf[rows, columns], h_buf[rows], (((0,), (0,)), ((), ())), preferred_element_type=jnp.float32
        )

    def wg(pair, start):
        first = pair_rows(pair)
        if start:
            loads[2].wait()

        def step(i, _):
            columns, block = product(first, i)
            if start:
                acc[columns] = block
            else:
                acc[columns] += block
            return 0

        lax.fori_loop(0, D // width, step, 0)

    def end(pair):
        first = pair_rows(pair)

        def out(i):
            columns = pl.ds(pl.multiple_of(i * width, width), width)
            return pltpu.make_async_copy(w_buf.at[columns], merged.at[0, columns], out_sem.at[i])

        def step(i, _):
            columns, block = product(first, i)
            w_buf[columns] = ((acc[columns] + block) * blend).astype(jnp.bfloat16)
            out(i).start()
            return 0

        lax.fori_loop(0, D // width, step, 0)
        for i in range(D // width):
            out(i).wait()

    tasks = {"reduce": reduce, "outer": outer, "relay": relay, "blend": blend_all, "hg": hg, "wg": wg, "end": end}
    steps, sent_rows, _ = plan()
    for step in steps:
        if step[0] == "send":
            passing(*step[1:]).start()
        elif step[0] == "wait":
            landed(step[1])
        else:
            tasks[step[1]](*step[2:])
    for copy in hg_copies[-2:]:
        copy.wait()
    ng_out.wait()
    nm_out.wait()
    for link, rows in enumerate(sent_rows):
        whole = c_buf.at[pl.ds(0, rows)]
        remote(whole, whole, send_sem.at[link], recv_sem.at[0, 0], partner[link]).wait_send()


def body(hidden, cotangent, local_weight, pending, global_weight, outer_momentum):
    big = jax.ShapeDtypeStruct((1, D, FF_SHARE), jnp.bfloat16)
    part = jax.ShapeDtypeStruct((D // islands, FF_SHARE), jnp.float32)
    slots = jax.ShapeDtypeStruct((D, FF_SHARE), jnp.bfloat16)
    outs = pl.pallas_call(
        kernel,
        out_shape=(big, big, part, part, slots),
        in_specs=[pl.BlockSpec(memory_space=pl.ANY)] * 6,
        out_specs=[pl.BlockSpec(memory_space=pl.ANY)] * 5,
        scratch_shapes=[
            pltpu.VMEM((TOKENS, D), jnp.bfloat16),
            pltpu.VMEM((TOKENS, FF_SHARE), jnp.bfloat16),
            pltpu.VMEM((D, FF_SHARE), jnp.bfloat16),
            pltpu.VMEM((D, FF_SHARE), jnp.float32),
            pltpu.VMEM((2, 2 * SHARD, FF_SHARE), jnp.bfloat16),
            pltpu.VMEM((2, 1024, FF_SHARE), jnp.bfloat16),
            pltpu.VMEM((2, 1024, FF_SHARE), jnp.bfloat16),
            pltpu.VMEM((1024, FF_SHARE), jnp.bfloat16),
            pltpu.VMEM((1024, FF_SHARE), jnp.float32),
            pltpu.VMEM((1024, FF_SHARE), jnp.float32),
            pltpu.SemaphoreType.DMA((len(LINKS),)),
            pltpu.SemaphoreType.DMA((32, len(PIECES))),
            pltpu.SemaphoreType.DMA((8,)),
            pltpu.SemaphoreType.DMA((2,)),
            pltpu.SemaphoreType.DMA((10,)),
            pltpu.SemaphoreType.DMA((6,)),
            pltpu.SemaphoreType.DMA((6,)),
        ],
        compiler_params=pltpu.CompilerParams(collective_id=0, has_side_effects=True, vmem_limit_bytes=63 * MIB),
        cost_estimate=pl.CostEstimate(flops=4 * TOKENS * D * FF_SHARE, bytes_accessed=64 * MIB, transcendentals=0),
        name="gather_and_update",
    )(hidden, cotangent, local_weight, pending, global_weight, outer_momentum)
    return outs[:4]


def solution(mesh):
    placed = (
        P("island", None, "mp"),
        P("island", "mp", None),
        P("island", None, "mp"),
        P("island", None, "mp"),
        P("island", "mp"),
        P("island", "mp"),
    )
    return jax.shard_map(
        body,
        mesh=mesh,
        in_specs=placed,
        out_specs=(
            P("island", None, "mp"),
            P("island", None, "mp"),
            P("island", "mp"),
            P("island", "mp"),
        ),
        check_vma=False,
    )
```

```python
import math

import jax
import jax.numpy as jnp
from jax import lax
from jax.experimental import pallas as pl
from jax.experimental.pallas import tpu as pltpu
from jax.sharding import PartitionSpec as P

D = 4096
TOKENS = 4096
FF_SHARE = 448
SHARD = 128

inner_rate = 0.3
outer_rate = 0.7
decay_rate = 0.9
mix_weight = 0.5
islands = 4

MESH = pl.DeviceIdType.MESH
MIB = 2**20

PIECES = (
    (0, 32, 0, True, 1),
    (32, 16, 0, True, -1),
    (48, 16, 0, False, -1),
    (64, 32, 1, True, 1),
    (96, 16, 1, True, -1),
    (112, 16, 1, False, -1),
)
LINKS = ((0, 1), (0, -1), (1, 1), (1, -1), (2, 1))
WRAP = (4, 4, 2)


def moved(offset, link):
    axis, step = LINKS[link]
    out = list(offset)
    out[axis] = (out[axis] + step) % WRAP[axis]
    return tuple(out)


def links_of(piece, offset):
    _, _, first, early, way = PIECES[piece]
    second = 1 - first
    found = []
    if offset[2] == 0 and (offset[first], offset[second]) == (0, 0) and early:
        found.append(4)
    if early or offset[2] == 0:
        for axis in (first, second):
            if axis == first and offset[second] != 0:
                continue
            turn = way if axis == first or offset[first] % 2 == 0 else -way
            for step in (1, -1):
                link = LINKS.index((axis, step))
                if offset[axis] == 0 or (offset[axis] == step % 4 and turn == step):
                    found.append(link)
    if offset[2] == 0 and not early:
        found.append(4)
    return found


def order_of(pair):
    dz, dx = min(pair[0], 4 - pair[0]), min(pair[1], 4 - pair[1])
    return (dz + dx, max(dz, dx), pair)


PAIRS = sorted(((dz, dx) for dz in range(4) for dx in range(4)), key=order_of)
FIRST_DUE, LAST_DUE, HOP = 30.0, 150.0, 6.0


def due_of(piece, offset):
    rank = PAIRS.index(offset[:2])
    best = FIRST_DUE + (LAST_DUE - FIRST_DUE) * rank / (len(PAIRS) - 1)
    for link in links_of(piece, offset):
        best = min(best, due_of(piece, moved(offset, link)) - HOP)
    return best


def plan():
    unit = 2.87 / 16
    latency = LATENCY
    hg_time, wg_time = TASK_TIMES
    heaps = [[] for _ in LINKS]
    free_at = [0.0] * len(LINKS)
    queued = [[] for _ in LINKS]
    arrivals = []
    steps = []
    have = {}
    now = 0.0
    sent_rows = [0] * len(LINKS)
    todo_hg, todo_wg = [], []
    islands_due = [(ISLAND_AT, "reduce")]
    island_rows = FF_SHARE // 4
    pieces = range(len(PIECES))
    due = {}
    finished = []

    def offer(item):
        for link in links_of(*item):
            after = (item[0], moved(item[1], link))
            if after not in due:
                due[after] = due_of(*after)
            heaps[link].append((due[after], item))

    def pump():
        for link in range(len(LINKS)):
            while True:
                queued[link] = [t for t in queued[link] if t > now]
                if len(queued[link]) >= DEPTH or not heaps[link]:
                    break
                heaps[link].sort()
                _, item = heaps[link].pop(0)
                rows = PIECES[item[0]][1]
                start = max(now, free_at[link])
                free_at[link] = start + unit * rows
                queued[link].append(free_at[link])
                sent_rows[link] += rows
                steps.append(("send", item, link))
                arrivals.append((free_at[link] + latency[link], (item[0], moved(item[1], link))))

    def land(item):
        have[item] = True
        pair = item[1][:2]
        if all((p, pair + (dy,)) in have for p in pieces for dy in (0, 1)):
            todo_hg.append(pair)
            todo_wg.append(pair)
            finished.append((round(now, 1), pair))

    for p in pieces:
        item = (p, (0, 0, 0))
        have[item] = True
        offer(item)
    pump()
    total = len(PIECES) * 32
    first_wg = True
    while len(have) < total or todo_hg or todo_wg or islands_due:
        arrivals.sort()
        while arrivals and arrivals[0][0] <= now:
            _, item = arrivals.pop(0)
            steps.append(("wait", item))
            land(item)
            offer(item)
            now += 0.06
        pump()
        if islands_due and islands_due[0][0] <= now and not (islands_due[0][1] == "blend" and first_wg):
            name = islands_due.pop(0)[1]
            steps.append(("task", name))
            now += 1.5
            if name in ("reduce", "outer"):
                free_at[4] = max(now, free_at[4]) + unit * island_rows
                queued[4].append(free_at[4])
                islands_due.append((free_at[4] + latency[4], "outer" if name == "reduce" else "relay"))
            elif name == "relay":
                islands_due.append((now + 12.0, "blend"))
        elif todo_hg and len(todo_hg) >= len(todo_wg):
            steps.append(("task", "hg", todo_hg.pop(0)))
            now += hg_time
        elif todo_wg:
            steps.append(("task", "wg", todo_wg.pop(0), first_wg))
            first_wg = False
            now += wg_time
        else:
            times = [t for t, _ in arrivals[:1]] + [t for t, _ in islands_due[:1]]
            for link, q in enumerate(queued):
                if len(q) >= DEPTH and heaps[link]:
                    times.append(min(q))
            times = [t for t in times if t > now]
            now = min(times) if times else now + 0.1
    last = max(i for i, s in enumerate(steps) if s[0] == "task" and s[1] == "wg")
    steps[last] = ("task", "end") + steps[last][2:3]
    return steps, sent_rows, now, finished


TASK_TIMES = (1.5, 1.5)
DEPTH = 2
LATENCY = (4.0, 4.0, 4.0, 4.0, 6.0)
ISLAND_AT = 16.0


def kernel(
    hidden, cotangent, local_weight, pending, global_weight, outer_momentum,
    hidden_grad, merged, new_global, new_momentum, fresh,
    c_buf, h_buf, w_buf, acc, hg_buf, p_buf, pc_buf, py_buf, g_buf, m_buf,
    send_sem, recv_sem, load_sem, hg_sem, out_sem, isl_send, isl_recv,
):
    island = lax.axis_index("island")
    mp = lax.axis_index("mp")
    z, x, yh = mp // 8, (mp // 2) % 4, mp % 2
    core, yl = island % 2, island // 2

    def mp_at(pz, px, py):
        return (lax.rem(pz, 4) * 4 + lax.rem(px, 4)) * 2 + lax.rem(py, 2)

    partner = [
        {"mp": mp_at(z + 1, x, yh)},
        {"mp": mp_at(z + 3, x, yh)},
        {"mp": mp_at(z, x + 1, yh)},
        {"mp": mp_at(z, x + 3, yh)},
        {"mp": mp_at(z, x, yh + 1)},
    ]
    other_core = {"island": yl * 2 + 1 - core}
    other_y = {"island": (1 - yl) * 2 + core}

    loads = [
        pltpu.make_async_copy(cotangent, c_buf.at[pl.ds(pl.multiple_of(mp * SHARD, SHARD), SHARD)], load_sem.at[0]),
        pltpu.make_async_copy(local_weight, w_buf, load_sem.at[1]),
        pltpu.make_async_copy(hidden, h_buf, load_sem.at[2]),
        pltpu.make_async_copy(global_weight, g_buf, load_sem.at[3]),
        pltpu.make_async_copy(outer_momentum, m_buf, load_sem.at[4]),
    ]

    def quarter(ref, index):
        return ref.at[:, pl.ds(pl.multiple_of(index * 1024, 1024), 1024)]

    mine, theirs = yl * 2 + core, (1 - yl) * 2 + core
    p_loads = [
        pltpu.make_async_copy(quarter(pending, theirs), p_buf.at[0], load_sem.at[5]),
        pltpu.make_async_copy(quarter(pending, mine), p_buf.at[1], load_sem.at[6]),
    ]
    for copy in loads + p_loads:
        copy.start()

    barrier = pltpu.get_barrier_semaphore()
    for device in partner + [other_core, other_y]:
        pl.semaphore_signal(barrier, inc=1, device_id=device, device_id_type=MESH)
    pl.semaphore_wait(barrier, len(partner) + 2)

    def rows_of(offset):
        dz, dx, dy = offset
        return mp_at(z + 4 - dz, x + 4 - dx, yh + dy) * SHARD

    def index_of(offset):
        return (offset[0] * 4 + offset[1]) * 2 + offset[2]

    def place(item):
        first, rows = PIECES[item[0]][:2]
        return c_buf.at[pl.ds(pl.multiple_of(rows_of(item[1]) + first, 16), rows)]

    def remote(src, dst, ssem, rsem, device):
        return pltpu.make_async_remote_copy(src, dst, ssem, rsem, device_id=device, device_id_type=MESH)

    def passing(item, link):
        dst = place(item)
        first, rows = PIECES[item[0]][:2]
        src = cotangent.at[pl.ds(first, rows)] if item[1] == (0, 0, 0) else dst
        return remote(src, dst, send_sem.at[link], recv_sem.at[index_of(moved(item[1], link)), item[0]], partner[link])

    def landed(item):
        dst = place(item)
        remote(dst, dst, send_sem.at[0], recv_sem.at[index_of(item[1]), item[0]], partner[0]).wait_recv()

    swap = [
        remote(quarter(pending, half * 2 + 1 - core), pc_buf.at[half], isl_send.at[half], isl_recv.at[half], other_core)
        for half in (0, 1)
    ]
    for copy in swap:
        copy.start()
    to_y = remote(p_buf.at[0], py_buf, isl_send.at[2], isl_recv.at[2], other_y)
    fresh_y = remote(p_buf.at[1], quarter(fresh, mine), isl_send.at[3], isl_recv.at[3], other_y)
    fresh_c = remote(p_buf.at[1], quarter(fresh, mine), isl_send.at[4], isl_recv.at[4], other_core)
    relay_c = remote(quarter(fresh, theirs), quarter(fresh, theirs), isl_send.at[5], isl_recv.at[5], other_core)
    ng_out = pltpu.make_async_copy(g_buf, new_global, out_sem.at[8])
    nm_out = pltpu.make_async_copy(m_buf, new_momentum, out_sem.at[9])

    backward_scale = 1.0 / math.sqrt(D)
    blend = -mix_weight * inner_rate / math.sqrt(TOKENS)
    tile = 64

    def reduce():
        for copy in p_loads:
            copy.wait()
        for copy in swap:
            copy.wait()

        def step(i, _):
            rows = pl.ds(pl.multiple_of(i * tile, tile), tile)
            p_buf[0, rows] = (p_buf[0, rows].astype(jnp.float32) + pc_buf[1 - yl, rows].astype(jnp.float32)).astype(jnp.bfloat16)
            return 0

        lax.fori_loop(0, FF_SHARE // tile, step, 0)
        to_y.start()

    def outer():
        loads[3].wait()
        loads[4].wait()
        to_y.wait()

        def step(i, _):
            rows = pl.ds(pl.multiple_of(i * tile, tile), tile)
            mean = (
                p_buf[1, rows].astype(jnp.float32) + pc_buf[yl, rows].astype(jnp.float32) + py_buf[rows].astype(jnp.float32)
            ) / islands
            momentum = decay_rate * m_buf[rows] + mean
            weight = g_buf[rows] - outer_rate * (mean + decay_rate * momentum)
            m_buf[rows] = momentum
            g_buf[rows] = weight
            p_buf[1, rows] = weight.astype(jnp.bfloat16)
            return 0

        lax.fori_loop(0, FF_SHARE // tile, step, 0)
        fresh_y.start()
        fresh_c.start()
        ng_out.start()
        nm_out.start()

    def relay():
        fresh_y.wait()
        relay_c.start()

    def add_base(source, index):
        columns = pl.ds(pl.multiple_of(index * 1024, 1024), 1024)

        def step(i, _):
            rows = pl.ds(pl.multiple_of(i * tile, tile), tile)
            base = mix_weight * w_buf[rows, columns].astype(jnp.float32) + (1.0 - mix_weight) * p_buf[source, rows].astype(
                jnp.float32
            )
            acc[rows, columns] += base * (1.0 / blend)
            return 0

        lax.fori_loop(0, FF_SHARE // tile, step, 0)

    def blend_all():
        fresh_c.wait()
        relay_c.wait()
        add_base(1, mine)
        for index in (theirs, yl * 2 + 1 - core, (1 - yl) * 2 + 1 - core):
            load = pltpu.make_async_copy(quarter(fresh, index), p_buf.at[0], load_sem.at[7])
            load.start()
            load.wait()
            add_base(0, index)

    def pair_tokens(pair):
        return pl.ds(pl.multiple_of(mp_at(z + 4 - pair[0], x + 4 - pair[1], 0) * SHARD, 2 * SHARD), 2 * SHARD)

    hg_copies = []

    def hg(pair):
        tokens = pair_tokens(pair)
        slot = len(hg_copies) % 2
        if len(hg_copies) == 0:
            loads[0].wait()
            loads[1].wait()
        if len(hg_copies) >= 2:
            hg_copies[-2].wait()
        block = lax.dot_general(
            w_buf[...], c_buf[tokens], (((1,), (1,)), ((), ())), preferred_element_type=jnp.float32
        )
        hg_buf[slot] = (block * backward_scale).astype(jnp.bfloat16)
        copy = pltpu.make_async_copy(hg_buf.at[slot], hidden_grad.at[:, tokens], hg_sem.at[slot])
        copy.start()
        hg_copies.append(copy)

    width = 512

    def product(tokens, i):
        columns = pl.ds(pl.multiple_of(i * width, width), width)
        return columns, jnp.dot(h_buf[:, tokens], c_buf[tokens, columns], preferred_element_type=jnp.float32)

    def wg(pair, start):
        tokens = pair_tokens(pair)
        if start:
            loads[2].wait()

        def step(i, _):
            columns, block = product(tokens, i)
            if start:
                acc[:, columns] = block
            else:
                acc[:, columns] += block
            return 0

        lax.fori_loop(0, D // width, step, 0)

    def end(pair):
        tokens = pair_tokens(pair)

        def out(i):
            columns = pl.ds(pl.multiple_of(i * width, width), width)
            return pltpu.make_async_copy(w_buf.at[:, columns], merged.at[:, columns], out_sem.at[i])

        def step(i, _):
            columns, block = product(tokens, i)
            w_buf[:, columns] = ((acc[:, columns] + block) * blend).astype(jnp.bfloat16)
            out(i).start()
            return 0

        lax.fori_loop(0, D // width, step, 0)
        for i in range(D // width):
            out(i).wait()

    tasks = {"reduce": reduce, "outer": outer, "relay": relay, "blend": blend_all, "hg": hg, "wg": wg, "end": end}
    steps, sent_rows = plan()[:2]
    for step in steps:
        if step[0] == "send":
            passing(*step[1:]).start()
        elif step[0] == "wait":
            landed(step[1])
        else:
            tasks[step[1]](*step[2:])
    for copy in hg_copies[-2:]:
        copy.wait()
    ng_out.wait()
    nm_out.wait()
    for link, rows in enumerate(sent_rows):
        whole = c_buf.at[pl.ds(0, rows)]
        remote(whole, whole, send_sem.at[link], recv_sem.at[0, 0], partner[link]).wait_send()


def body(hidden, cotangent, local_weight, pending, global_weight, outer_momentum):
    big = jax.ShapeDtypeStruct((FF_SHARE, D), jnp.bfloat16)
    part = jax.ShapeDtypeStruct((FF_SHARE, D // islands), jnp.float32)
    outs = pl.pallas_call(
        kernel,
        out_shape=(big, big, part, part, big),
        in_specs=[pl.BlockSpec(memory_space=pl.ANY)] * 6,
        out_specs=[pl.BlockSpec(memory_space=pl.ANY)] * 5,
        scratch_shapes=[
            pltpu.VMEM((TOKENS, D), jnp.bfloat16),
            pltpu.VMEM((FF_SHARE, TOKENS), jnp.bfloat16),
            pltpu.VMEM((FF_SHARE, D), jnp.bfloat16),
            pltpu.VMEM((FF_SHARE, D), jnp.float32),
            pltpu.VMEM((2, FF_SHARE, 2 * SHARD), jnp.bfloat16),
            pltpu.VMEM((2, FF_SHARE, 1024), jnp.bfloat16),
            pltpu.VMEM((2, FF_SHARE, 1024), jnp.bfloat16),
            pltpu.VMEM((FF_SHARE, 1024), jnp.bfloat16),
            pltpu.VMEM((FF_SHARE, 1024), jnp.float32),
            pltpu.VMEM((FF_SHARE, 1024), jnp.float32),
            pltpu.SemaphoreType.DMA((len(LINKS),)),
            pltpu.SemaphoreType.DMA((32, len(PIECES))),
            pltpu.SemaphoreType.DMA((8,)),
            pltpu.SemaphoreType.DMA((2,)),
            pltpu.SemaphoreType.DMA((10,)),
            pltpu.SemaphoreType.DMA((6,)),
            pltpu.SemaphoreType.DMA((6,)),
        ],
        compiler_params=pltpu.CompilerParams(collective_id=0, has_side_effects=True, vmem_limit_bytes=62 * MIB),
        cost_estimate=pl.CostEstimate(flops=4 * TOKENS * D * FF_SHARE, bytes_accessed=64 * MIB, transcendentals=0),
        name="gather_and_update",
    )(hidden[0].T, cotangent[0], local_weight[0].T, pending[0].T, global_weight.T, outer_momentum.T)
    return outs[0].T[None], outs[1].T[None], outs[2].T, outs[3].T


def solution(mesh):
    placed = (
        P("island", None, "mp"),
        P("island", "mp", None),
        P("island", None, "mp"),
        P("island", None, "mp"),
        P("island", "mp"),
        P("island", "mp"),
    )
    return jax.shard_map(
        body,
        mesh=mesh,
        in_specs=placed,
        out_specs=(
            P("island", None, "mp"),
            P("island", None, "mp"),
            P("island", "mp"),
            P("island", "mp"),
        ),
        check_vma=False,
    )
```

```python
import math

import jax
import jax.numpy as jnp
from jax import lax
from jax.experimental import pallas as pl
from jax.experimental.pallas import tpu as pltpu
from jax.sharding import PartitionSpec as P

D = 4096
TOKENS = 4096
FF_SHARE = 448
SHARD = 128
HALF = FF_SHARE // 2
CUT = 2048

inner_rate = 0.3
outer_rate = 0.7
decay_rate = 0.9
mix_weight = 0.5
islands = 4

MESH = pl.DeviceIdType.MESH
MIB = 2**20

KINDS = (((0, 64), (0, 0)), ((0, 32), (32, 32)))
SPANS = ((0, CUT), (CUT, D - CUT))
LINKS = ((0, 1), (0, -1), (1, 2), (2, 1))
WRAP = (4, 4, 2)
ORIGIN = (0, 0, 0)
OFFSETS = tuple((dz, dx, dy) for dz in range(4) for dx in range(4) for dy in range(2))


def moved(offset, link):
    axis, step = LINKS[link]
    out = list(offset)
    out[axis] = (out[axis] + step) % WRAP[axis]
    return tuple(out)


def links_of(kind, offset):
    dz, dx, dy = offset
    found = []
    if offset == ORIGIN:
        found.append(2)
    if kind == 0 and dz == 0 and dy == 0:
        found.append(3)
    if kind == 1 and dy == 0:
        found.append(3)
    if kind == 0 or dy == 0:
        way = 1 if (dx + dy) % 2 == 0 else -1
        if dz == 0 or (dz == 1 and way == 1):
            found.append(0)
        if dz == 0 or (dz == 3 and way == -1):
            found.append(1)
    return found


def order_of(pair):
    dz, dx = min(pair[0], 4 - pair[0]), min(pair[1], 4 - pair[1])
    return (dz, dx, pair)


PAIRS = sorted(((dz, dx) for dz in range(4) for dx in range(4)), key=order_of)
DUE = ((24.0, 65.8), (59.8, 72.9))
HOP = 3.0
ORDER = ("hg0", "wg0", "hg1", "wg1")
TASK_TIMES = ((1.0, 0.83), (1.15, 0.83))
DEPTH = 2
LATENCY = (4.0, 4.0, 5.0, 6.0)
ISLAND_AT = 7.0
SWAP_AT = (18.0, 36.0)
WORK_AT = (46.0, 64.0)
SPECIAL_AT = (18.0, 26.0)


def due_of(span, kind, offset):
    first, last = DUE[span]
    best = first + (last - first) * PAIRS.index(offset[:2]) / (len(PAIRS) - 1)
    for link in links_of(kind, offset):
        best = min(best, due_of(span, kind, moved(offset, link)) - HOP)
    return best


def plan():
    per_kib = 22.4 / 1024
    heaps = [[] for _ in LINKS]
    free_at = [0.0, 0.0, 8.0, 0.0]
    queued = [[] for _ in LINKS]
    arrivals = []
    steps = []
    have = set()
    sent_rows = [[0, 0] for _ in LINKS]
    state = {"now": 0.0}
    todo = {"hg0": [], "wg0": [], "hg1": [], "wg1": []}
    done = {"hg0": set(), "wg0": set(), "hg1": set(), "wg1": set()}
    flags = set()
    due_tasks = [(SWAP_AT[0], "swap_w"), (SWAP_AT[1], "swap_h"), (ISLAND_AT, "reduce")]
    island_kib = FF_SHARE * 2
    finished = []

    def offer(span, kind, offset):
        for link in links_of(kind, offset) if KINDS[span][kind][1] else ():
            heaps[link].append((due_of(span, kind, moved(offset, link)), span, kind, offset))

    def pump():
        now = state["now"]
        for link in range(len(LINKS)):
            while True:
                queued[link] = [t for t in queued[link] if t > now]
                if len(queued[link]) >= DEPTH or not heaps[link]:
                    break
                heaps[link].sort()
                _, span, kind, offset = heaps[link].pop(0)
                rows = KINDS[span][kind][1]
                start = max(now, free_at[link])
                free_at[link] = start + per_kib * rows * SPANS[span][1] / 512
                queued[link].append(free_at[link])
                sent_rows[link][span] += rows
                steps.append(("send", span, kind, offset, link))
                arrivals.append((free_at[link] + LATENCY[link], "wait", span, kind, moved(offset, link)))

    def check(span, offset):
        pair = offset[:2]
        if all((w, span, k, pair + (dy,)) in have for w in ("wait", "other") for k in (0, 1) for dy in (0, 1)):
            todo[f"hg{span}"].append(pair)
            todo[f"wg{span}"].append(pair)
            finished.append((round(state["now"], 1), span, pair))

    def land(entry):
        _, what, span, kind, offset = entry
        state["now"] += 0.06
        if what == "other":
            steps.append(("other", span, offset))
            have.update({("other", span, 0, offset), ("other", span, 1, offset)})
        else:
            steps.append(("wait", span, kind, offset))
            have.add(("wait", span, kind, offset))
            if not KINDS[span][1 - kind][1]:
                have.add(("wait", span, 1 - kind, offset))
            offer(span, kind, offset)
            if ("wait", span, 1 - kind, offset) in have:
                steps.append(("across", span, offset))
                arrivals.append((state["now"] + 4.0, "other", span, 0, offset))
        check(span, offset)

    for span in (0, 1):
        steps.append(("seed", span))
        for kind in (0, 1):
            have.update({("wait", span, kind, ORIGIN), ("other", span, kind, ORIGIN)})
            offer(span, kind, ORIGIN)
            for dx in (1, 3) if KINDS[span][kind][1] else ():
                arrivals.append((SPECIAL_AT[span], "wait", span, kind, (0, dx, 0)))
    pump()
    total = 2 * 2 * 2 * 32
    while True:
        arrivals.sort()
        while arrivals and arrivals[0][0] <= state["now"]:
            land(arrivals.pop(0))
            arrivals.sort()
        pump()
        due_tasks.sort()
        now = state["now"]
        ready = None
        for name in ORDER:
            if now < WORK_AT[name[0] == "w"] or not todo[name]:
                continue
            options = [p for p in todo[name] if name != "hg1" or p in done["hg0"]]
            if name[0] == "w":
                options = [p for p in options if p in done["h" + name[1:]]]
            if options:
                ready = (name, options[0])
                break
        if due_tasks and due_tasks[0][0] <= now and not (due_tasks[0][1] == "blend" and not done["wg0"]):
            name = due_tasks.pop(0)[1]
            steps.append(("task", name) + ((len(done["wg1"]) > 0,) if name == "blend" else ()))
            flags.add(name)
            state["now"] += 1.5
            if name in ("reduce", "outer"):
                free_at[3] = max(state["now"], free_at[3]) + per_kib * island_kib
                queued[3].append(free_at[3])
                due_tasks.append((free_at[3] + LATENCY[3], "outer" if name == "reduce" else "relay"))
            elif name == "relay":
                due_tasks.append((state["now"] + 8.0, "lend"))
            elif name == "lend":
                due_tasks.append((max(state["now"] + 26.0, WORK_AT[1] + 4.0), "blend"))
        elif len(done["wg0"]) == len(PAIRS) and "blend" in flags and "end0" not in flags:
            steps.append(("task", "end0"))
            flags.add("end0")
            state["now"] += 2.0
        elif ready:
            name, pair = ready
            took = options[:2] if name[0] == "w" else pair
            steps.append(("task", name[:2], int(name[2]), took, not done[name] and not (name == "wg1" and "blend" in flags)))
            for one in took if name[0] == "w" else [pair]:
                todo[name].remove(one)
                done[name].add(one)
                state["now"] += TASK_TIMES[int(name[2])][name[0] == "w"]
        elif len(have) == total and len(done["wg1"]) == len(PAIRS) and not due_tasks:
            break
        else:
            times = [t[0] for t in arrivals[:1]] + [t[0] for t in due_tasks]
            for link, q in enumerate(queued):
                if len(q) >= DEPTH and heaps[link]:
                    times.append(min(q))
            times = [t for t in times if t > now]
            state["now"] = min(times) if times else now + 0.1
            if len(have) == total and len(done["wg1"]) == len(PAIRS):
                break
    while due_tasks:
        steps.append(("task", due_tasks.pop(0)[1]))
    last = max(i for i, s in enumerate(steps) if s[0] == "task" and s[1] == "wg")
    steps[last] = ("task", "end1", steps[last][3])
    return steps, sent_rows, state["now"], finished


def kernel(
    hidden, cotangent, local_weight, pending, global_weight, outer_momentum,
    hidden_grad, merged, new_global, new_momentum, fresh, lent,
    c_lo, c_hi, h_buf, w_buf, acc, part, p_buf, pc_buf, py_buf, g_buf, m_buf,
    send_sem, mine_sem, across_sem, other_sem, seed_sem, special_sem, swap_send, swap_recv,
    load_sem, hg_sem, hg_send, hg_recv, out_sem, back_send, back_recv, isl_send, isl_recv,
):
    island = lax.axis_index("island")
    mp = lax.axis_index("mp")
    z, x, yh = mp // 8, (mp // 2) % 4, mp % 2
    core, yl = island % 2, island // 2
    role = lax.rem(core + x, 2)
    c_bufs = (c_lo, c_hi)

    def mp_at(pz, px, py):
        return (lax.rem(pz, 4) * 4 + lax.rem(px, 4)) * 2 + lax.rem(py, 2)

    partner = [
        {"mp": mp_at(z + 1, x, yh)},
        {"mp": mp_at(z + 3, x, yh)},
        {"mp": mp_at(z, x + 2, yh)},
        {"mp": mp_at(z, x, yh + 1)},
    ]
    other_core = {"island": yl * 2 + 1 - core}
    other_y = {"island": (1 - yl) * 2 + core}

    def beside(step, its_role):
        return {"island": yl * 2 + lax.rem(x + 1 + its_role, 2), "mp": mp_at(z, x + step, yh)}

    def only(which, action):
        pl.when(role == which)(action)

    def remote(src, dst, ssem, rsem, device):
        return pltpu.make_async_remote_copy(src, dst, ssem, rsem, device_id=device, device_id_type=MESH)

    def quarter(ref, index):
        return ref.at[:, pl.ds(pl.multiple_of(index * 1024, 1024), 1024)]

    def half(index):
        return pl.ds(index * HALF, HALF)

    own = [
        pltpu.make_async_copy(
            cotangent.at[:, pl.ds(*SPANS[span])],
            c_bufs[span].at[pl.ds(pl.multiple_of(mp * SHARD, SHARD), SHARD)],
            load_sem.at[span],
        )
        for span in (0, 1)
    ]
    w_load = pltpu.make_async_copy(local_weight, w_buf, load_sem.at[2])
    h_load = pltpu.make_async_copy(hidden, h_buf, load_sem.at[3])
    g_load = pltpu.make_async_copy(global_weight, g_buf, load_sem.at[4])
    m_load = pltpu.make_async_copy(outer_momentum, m_buf, load_sem.at[5])
    mine, theirs = yl * 2 + core, (1 - yl) * 2 + core
    p_loads = [
        pltpu.make_async_copy(quarter(pending, theirs), p_buf.at[0], load_sem.at[6]),
        pltpu.make_async_copy(quarter(pending, mine), p_buf.at[1], load_sem.at[7]),
    ]

    @pl.when(role == 0)
    def _():
        for copy in own + [w_load, h_load]:
            copy.start()

    for copy in p_loads + [g_load, m_load]:
        copy.start()

    barrier = pltpu.get_barrier_semaphore()
    greeted = partner + [other_core, other_y] + [beside(step, r) for step in (1, 3) for r in (0, 1)]
    for device in greeted:
        pl.semaphore_signal(barrier, inc=1, device_id=device, device_id_type=MESH)
    pl.semaphore_wait(barrier, len(greeted))

    def index_of(offset):
        return (offset[0] * 4 + offset[1]) * 2 + offset[2]

    def rows_of(offset):
        dz, dx, dy = offset
        return mp_at(z + 4 - dz, x + 4 - dx, yh + dy) * SHARD

    def place(span, kind, offset, side):
        first, rows = KINDS[span][kind]
        return c_bufs[span].at[pl.ds(pl.multiple_of(rows_of(offset) + side * 64 + first, 16), rows)]

    def place_all(span, offset, side):
        return c_bufs[span].at[pl.ds(pl.multiple_of(rows_of(offset) + side * 64, 16), 64)]

    def send(span, kind, offset, link):
        ref = place(span, kind, offset, role)
        remote(
            ref, ref, send_sem.at[link, span], mine_sem.at[span, kind, index_of(moved(offset, link))], partner[link]
        ).start()

    def wait(span, kind, offset):
        ref = place(span, kind, offset, role)
        remote(ref, ref, send_sem.at[0, span], mine_sem.at[span, kind, index_of(offset)], partner[0]).wait_recv()

    def across(span, offset):
        ref = place_all(span, offset, role)
        remote(ref, ref, across_sem.at[span], other_sem.at[span, index_of(offset)], other_core).start()

    def other(span, offset):
        ref = place_all(span, offset, 1 - role)
        remote(ref, ref, across_sem.at[span], other_sem.at[span, index_of(offset)], other_core).wait_recv()

    def seed_copy(span):
        ref = c_bufs[span].at[pl.ds(pl.multiple_of(mp * SHARD, SHARD), SHARD)]
        return remote(ref, ref, seed_sem.at[0, span], seed_sem.at[1, span], other_core)

    def specials(span):
        for kind in (0, 1):
            first, rows = KINDS[span][kind]
            if not rows:
                continue
            for side in (0, 1):
                src = cotangent.at[pl.ds(side * 64 + first, rows), pl.ds(*SPANS[span])]
                dst = place(span, kind, ORIGIN, side)
                for step in (1, 3):
                    remote(
                        src, dst, special_sem.at[span], mine_sem.at[span, kind, index_of((0, step, 0))], beside(step, side)
                    ).start()

    def seed(span):
        @pl.when(role == 0)
        def _():
            own[span].wait()
            seed_copy(span).start()

        @pl.when(role == 1)
        def _():
            specials(span)
            seed_copy(span).wait_recv()

    swaps = [
        remote(source.at[half(i)], target.at[half(i)], swap_send.at[j, i], swap_recv.at[j, i], beside((1, 3)[i], 1))
        for j, (source, target) in enumerate(((local_weight, w_buf), (hidden, h_buf)))
        for i in (0, 1)
    ]

    def swap(which):
        @pl.when(role == 1)
        def _():
            for copy in swaps[2 * which : 2 * which + 2]:
                copy.start()

    pair_sum = [
        remote(quarter(pending, i * 2 + 1 - core), pc_buf.at[i], isl_send.at[i], isl_recv.at[i], other_core) for i in (0, 1)
    ]
    for copy in pair_sum:
        copy.start()
    to_y = remote(p_buf.at[0], py_buf, isl_send.at[2], isl_recv.at[2], other_y)
    fresh_y = remote(p_buf.at[1], quarter(fresh, mine), isl_send.at[3], isl_recv.at[3], other_y)
    fresh_c = remote(p_buf.at[1], quarter(fresh, mine), isl_send.at[4], isl_recv.at[4], other_core)
    relay_c = remote(quarter(fresh, theirs), quarter(fresh, theirs), isl_send.at[5], isl_recv.at[5], other_core)
    fresh_own = pltpu.make_async_copy(p_buf.at[1], quarter(fresh, mine), out_sem.at[4])
    ng_out = pltpu.make_async_copy(g_buf, new_global, out_sem.at[0])
    nm_out = pltpu.make_async_copy(m_buf, new_momentum, out_sem.at[1])

    backward_scale = 1.0 / math.sqrt(D)
    blend = -mix_weight * inner_rate / math.sqrt(TOKENS)
    tile = 64

    def by_tile(step):
        def one(i, _):
            step(pl.ds(pl.multiple_of(i * tile, tile), tile))
            return 0

        lax.fori_loop(0, FF_SHARE // tile, one, 0)

    def wide(value):
        return value.astype(jnp.float32)

    def reduce():
        for copy in p_loads + pair_sum:
            copy.wait()

        def step(rows):
            p_buf[0, rows] = (wide(p_buf[0, rows]) + wide(pc_buf[1 - yl, rows])).astype(jnp.bfloat16)

        by_tile(step)
        to_y.start()

    def outer():
        g_load.wait()
        m_load.wait()
        to_y.wait()

        def step(rows):
            mean = (wide(p_buf[1, rows]) + wide(pc_buf[yl, rows]) + wide(py_buf[rows])) / islands
            momentum = decay_rate * m_buf[rows] + mean
            weight = g_buf[rows] - outer_rate * (mean + decay_rate * momentum)
            m_buf[rows] = momentum
            g_buf[rows] = weight
            p_buf[1, rows] = weight.astype(jnp.bfloat16)

        by_tile(step)
        for copy in (fresh_y, fresh_c, fresh_own, ng_out, nm_out):
            copy.start()

    def relay():
        fresh_y.wait()
        relay_c.start()

    lends = [remote(fresh.at[half(i)], lent.at[half(i)], back_send.at[2, i], back_recv.at[2, i], beside((1, 3)[i], 1)) for i in (0, 1)]

    def lend():
        fresh_c.wait()
        fresh_own.wait()
        relay_c.wait()

        @pl.when(role == 1)
        def _():
            for copy in lends:
                copy.start()

    def fresh_load(source, index, slot):
        return pltpu.make_async_copy(quarter(source, index), p_buf.at[slot], load_sem.at[8 + slot])

    def start_fresh(index, slot):
        only(0, fresh_load(fresh, index, slot).start)
        only(1, fresh_load(lent, index, slot).start)

    def blend_all(started):
        @pl.when(role == 1)
        def _():
            for copy in lends:
                copy.wait()

        start_fresh(0, 0)
        for index in range(4):
            slot = index % 2
            fresh_load(fresh, index, slot).wait()
            if index < 3:
                start_fresh(index + 1, 1 - slot)

            def step(rows, slot=slot, index=index):
                for side in (0, 1):
                    first = index * 1024 + side * 512
                    columns = pl.ds(first, 512)
                    base = mix_weight * wide(w_buf[rows, columns]) + (1.0 - mix_weight) * wide(
                        p_buf[slot, rows, pl.ds(side * 512, 512)]
                    )
                    base = base * (1.0 / blend)
                    if first < CUT or started:
                        base = base + acc[rows, columns]
                    acc[rows, columns] = base

            by_tile(step)

    def pair_tokens(pair):
        return pl.ds(pl.multiple_of(mp_at(z + 4 - pair[0], x + 4 - pair[1], 0) * SHARD, 2 * SHARD), 2 * SHARD)

    def hg_out(tokens):
        return pltpu.make_async_copy(part.at[:, tokens], hidden_grad.at[:, tokens], hg_sem.at[0])

    def hg_back(i, tokens):
        return remote(
            part.at[half(i), tokens], hidden_grad.at[half(i), tokens], hg_send.at[i], hg_recv.at[i], beside((3, 1)[i], 1)
        )

    def hg(span, pair, start):
        tokens = pair_tokens(pair)
        if span == 0 and start:
            only(0, w_load.wait)

            @pl.when(role == 1)
            def _():
                for copy in swaps[:2]:
                    copy.wait()

        first, columns = SPANS[span]
        block = lax.dot_general(
            w_buf[:, pl.ds(first, columns)],
            c_bufs[span][tokens],
            (((1,), (1,)), ((), ())),
            preferred_element_type=jnp.float32,
        )
        if span == 0:
            part[:, tokens] = (block * backward_scale).astype(jnp.bfloat16)
            return
        part[:, tokens] = (wide(part[:, tokens]) + block * backward_scale).astype(jnp.bfloat16)

        @pl.when(role == 0)
        def _():
            hg_out(tokens).start()

        @pl.when(role == 1)
        def _():
            for i in (0, 1):
                hg_back(i, tokens).start()

    width = 512

    def product(span, pairs, i):
        columns = pl.ds(pl.multiple_of(i * width, width), width)
        there = pl.ds(pl.multiple_of(SPANS[span][0] + i * width, width), width)
        total = None
        for pair in pairs:
            tokens = pair_tokens(pair)
            block = jnp.dot(h_buf[:, tokens], c_bufs[span][tokens, columns], preferred_element_type=jnp.float32)
            total = block if total is None else total + block
        return there, total

    def wg(span, pairs, start):
        if span == 0 and start:
            only(0, h_load.wait)

            @pl.when(role == 1)
            def _():
                for copy in swaps[2:]:
                    copy.wait()

        def step(i, _):
            there, total = product(span, pairs, i)
            acc[:, there] = total if start else acc[:, there] + total
            return 0

        lax.fori_loop(0, SPANS[span][1] // width, step, 0)

    lo, hi = pl.ds(0, CUT), pl.ds(CUT, D - CUT)
    out_lo = pltpu.make_async_copy(w_buf.at[:, lo], merged.at[:, lo], out_sem.at[2])
    out_hi = pltpu.make_async_copy(w_buf.at[:, hi], merged.at[:, hi], out_sem.at[3])
    back_lo, back_hi = (
        [
            remote(
                w_buf.at[half(i), span], merged.at[half(i), span], back_send.at[j, i], back_recv.at[j, i], beside((3, 1)[i], 1)
            )
            for i in (0, 1)
        ]
        for j, span in enumerate((lo, hi))
    )

    def end0():
        def step(i, _):
            columns = pl.ds(pl.multiple_of(i * width, width), width)
            w_buf[:, columns] = (acc[:, columns] * blend).astype(jnp.bfloat16)
            return 0

        lax.fori_loop(0, CUT // width, step, 0)
        only(0, out_lo.start)

        @pl.when(role == 1)
        def _():
            for copy in back_lo:
                copy.start()

    def end1(pairs):
        def step(i, _):
            there, total = product(1, pairs, i)
            w_buf[:, there] = ((acc[:, there] + total) * blend).astype(jnp.bfloat16)
            return 0

        lax.fori_loop(0, (D - CUT) // width, step, 0)
        only(0, out_hi.start)

        @pl.when(role == 1)
        def _():
            for copy in back_hi:
                copy.start()

    def finish1():
        @pl.when(role == 0)
        def _():
            out_lo.wait()
            out_hi.wait()
            hg_out(pl.ds(0, TOKENS)).wait()

        @pl.when(role == 1)
        def _():
            for copy in back_lo + back_hi:
                copy.wait()
            for i in (0, 1):
                hg_back(i, pl.ds(0, TOKENS)).wait()

    tasks = {
        "swap_w": lambda: swap(0), "swap_h": lambda: swap(1), "reduce": reduce, "outer": outer, "relay": relay, "lend": lend, "blend": blend_all,
        "hg": hg, "wg": wg, "end0": end0, "end1": end1,
    }
    moves = {"seed": seed, "send": send, "wait": wait, "across": across, "other": other}
    steps, sent_rows = plan()[:2]
    for step in steps:
        if step[0] == "task":
            tasks[step[1]](*step[2:])
        else:
            if step[0] == "other" and step[2] == ORIGIN:
                continue
            moves[step[0]](*step[1:])
    finish1()
    ng_out.wait()
    nm_out.wait()
    for span in (0, 1):
        for link in range(len(LINKS)):
            whole = c_bufs[span].at[pl.ds(0, sent_rows[link][span])]
            remote(whole, whole, send_sem.at[link, span], mine_sem.at[0, 0, 0], partner[link]).wait_send()
        whole = c_bufs[span].at[pl.ds(0, 31 * 64)]
        remote(whole, whole, across_sem.at[span], other_sem.at[span, 0], other_core).wait_send()
        only(0, seed_copy(span).wait_send)

        @pl.when(role == 1)
        def _():
            whole = c_bufs[span].at[pl.ds(0, 2 * SHARD)]
            remote(whole, whole, special_sem.at[span], mine_sem.at[0, 0, 0], beside(1, 1)).wait_send()


def body(hidden, cotangent, local_weight, pending, global_weight, outer_momentum):
    big = jax.ShapeDtypeStruct((FF_SHARE, D), jnp.bfloat16)
    state = jax.ShapeDtypeStruct((FF_SHARE, D // islands), jnp.float32)
    dma = pltpu.SemaphoreType.DMA
    outs = pl.pallas_call(
        kernel,
        out_shape=(big, big, state, state, big, big),
        in_specs=[pl.BlockSpec(memory_space=pl.ANY)] * 6,
        out_specs=[pl.BlockSpec(memory_space=pl.ANY)] * 6,
        scratch_shapes=[
            pltpu.VMEM((TOKENS, CUT), jnp.bfloat16),
            pltpu.VMEM((TOKENS, D - CUT), jnp.bfloat16),
            pltpu.VMEM((FF_SHARE, TOKENS), jnp.bfloat16),
            pltpu.VMEM((FF_SHARE, D), jnp.bfloat16),
            pltpu.VMEM((FF_SHARE, D), jnp.float32),
            pltpu.VMEM((FF_SHARE, TOKENS), jnp.bfloat16),
            pltpu.VMEM((2, FF_SHARE, 1024), jnp.bfloat16),
            pltpu.VMEM((2, FF_SHARE, 1024), jnp.bfloat16),
            pltpu.VMEM((FF_SHARE, 1024), jnp.bfloat16),
            pltpu.VMEM((FF_SHARE, 1024), jnp.float32),
            pltpu.VMEM((FF_SHARE, 1024), jnp.float32),
            dma((len(LINKS), 2)),
            dma((2, 2, 32)),
            dma((2,)),
            dma((2, 32)),
            dma((2, 2)),
            dma((2,)),
            dma((2, 2)),
            dma((2, 2)),
            dma((14,)),
            dma((1,)),
            dma((2,)),
            dma((2,)),
            dma((5,)),
            dma((3, 2)),
            dma((3, 2)),
            dma((6,)),
            dma((6,)),
        ],
        compiler_params=pltpu.CompilerParams(collective_id=0, has_side_effects=True, vmem_limit_bytes=63 * MIB),
        cost_estimate=pl.CostEstimate(flops=4 * TOKENS * D * FF_SHARE, bytes_accessed=64 * MIB, transcendentals=0),
        name="gather_and_update",
    )(hidden[0].T, cotangent[0], local_weight[0].T, pending[0].T, global_weight.T, outer_momentum.T)
    return outs[0].T[None], outs[1].T[None], outs[2].T, outs[3].T


def solution(mesh):
    placed = (
        P("island", None, "mp"),
        P("island", "mp", None),
        P("island", None, "mp"),
        P("island", None, "mp"),
        P("island", "mp"),
        P("island", "mp"),
    )
    return jax.shard_map(
        body,
        mesh=mesh,
        in_specs=placed,
        out_specs=(
            P("island", None, "mp"),
            P("island", None, "mp"),
            P("island", "mp"),
            P("island", "mp"),
        ),
        check_vma=False,
    )
```

```python
import math

import jax
import jax.numpy as jnp
from jax import lax
from jax.experimental import pallas as pl
from jax.experimental.pallas import tpu as pltpu
from jax.sharding import PartitionSpec as P

D = 4096
TOKENS = 4096
FF_SHARE = 448
SHARD = 128
HALF = FF_SHARE // 2
CUT = 2048

inner_rate = 0.3
outer_rate = 0.7
decay_rate = 0.9
mix_weight = 0.5
islands = 4

MESH = pl.DeviceIdType.MESH
MIB = 2**20

KINDS = (((0, 64), (0, 0)), ((0, 32), (32, 32)))
SPANS = ((0, CUT), (CUT, D - CUT))
LINKS = ((0, 1), (0, -1), (1, 2), (2, 1))
WRAP = (4, 4, 2)
ORIGIN = (0, 0, 0)
OFFSETS = tuple((dz, dx, dy) for dz in range(4) for dx in range(4) for dy in range(2))


def moved(offset, link):
    axis, step = LINKS[link]
    out = list(offset)
    out[axis] = (out[axis] + step) % WRAP[axis]
    return tuple(out)


def links_of(kind, offset):
    dz, dx, dy = offset
    found = []
    if offset == ORIGIN:
        found.append(2)
    if kind == 0 and dz == 0 and dy == 0:
        found.append(3)
    if kind == 1 and dy == 0:
        found.append(3)
    if kind == 0 or dy == 0:
        way = 1 if (dx + dy) % 2 == 0 else -1
        if dz == 0 or (dz == 1 and way == 1):
            found.append(0)
        if dz == 0 or (dz == 3 and way == -1):
            found.append(1)
    return found


def order_of(pair):
    dz, dx = min(pair[0], 4 - pair[0]), min(pair[1], 4 - pair[1])
    return (dz, dx, pair)


PAIRS = sorted(((dz, dx) for dz in range(4) for dx in range(4)), key=order_of)
DUE = ((24.0, 65.8), (59.8, 72.9))
HOP = 3.0
ORDER = ("hg0", "wg0", "hg1", "wg1")
TASK_TIMES = ((1.0, 0.83), (1.15, 0.83))
DEPTH = 2
LATENCY = (4.0, 4.0, 5.0, 6.0)
ISLAND_AT = 7.0
SWAP_AT = (18.0, 36.0)
WORK_AT = (46.0, 64.0)
SPECIAL_AT = (18.0, 26.0)


def due_of(span, kind, offset):
    first, last = DUE[span]
    best = first + (last - first) * PAIRS.index(offset[:2]) / (len(PAIRS) - 1)
    for link in links_of(kind, offset):
        best = min(best, due_of(span, kind, moved(offset, link)) - HOP)
    return best


def plan():
    per_kib = 22.4 / 1024
    heaps = [[] for _ in LINKS]
    free_at = [0.0, 0.0, 8.0, 0.0]
    queued = [[] for _ in LINKS]
    arrivals = []
    steps = []
    have = set()
    sent_rows = [[0, 0] for _ in LINKS]
    state = {"now": 0.0}
    todo = {"hg0": [], "wg0": [], "hg1": [], "wg1": []}
    done = {"hg0": set(), "wg0": set(), "hg1": set(), "wg1": set()}
    flags = set()
    due_tasks = [(SWAP_AT[0], "swap_w"), (SWAP_AT[1], "swap_h"), (ISLAND_AT, "reduce")]
    island_kib = FF_SHARE * 2
    finished = []

    def offer(span, kind, offset):
        for link in links_of(kind, offset) if KINDS[span][kind][1] else ():
            heaps[link].append((due_of(span, kind, moved(offset, link)), span, kind, offset))

    def pump():
        now = state["now"]
        for link in range(len(LINKS)):
            while True:
                queued[link] = [t for t in queued[link] if t > now]
                if len(queued[link]) >= DEPTH or not heaps[link]:
                    break
                heaps[link].sort()
                _, span, kind, offset = heaps[link].pop(0)
                rows = KINDS[span][kind][1]
                start = max(now, free_at[link])
                free_at[link] = start + per_kib * rows * SPANS[span][1] / 512
                queued[link].append(free_at[link])
                sent_rows[link][span] += rows
                steps.append(("send", span, kind, offset, link))
                arrivals.append((free_at[link] + LATENCY[link], "wait", span, kind, moved(offset, link)))

    def check(span, offset):
        pair = offset[:2]
        if all((w, span, k, pair + (dy,)) in have for w in ("wait", "other") for k in (0, 1) for dy in (0, 1)):
            todo[f"hg{span}"].append(pair)
            todo[f"wg{span}"].append(pair)
            finished.append((round(state["now"], 1), span, pair))

    def land(entry):
        _, what, span, kind, offset = entry
        state["now"] += 0.06
        if what == "other":
            steps.append(("other", span, offset))
            have.update({("other", span, 0, offset), ("other", span, 1, offset)})
        else:
            steps.append(("wait", span, kind, offset))
            have.add(("wait", span, kind, offset))
            if not KINDS[span][1 - kind][1]:
                have.add(("wait", span, 1 - kind, offset))
            offer(span, kind, offset)
            if ("wait", span, 1 - kind, offset) in have:
                steps.append(("across", span, offset))
                arrivals.append((state["now"] + 4.0, "other", span, 0, offset))
        check(span, offset)

    for span in (0, 1):
        steps.append(("seed", span))
        for kind in (0, 1):
            have.update({("wait", span, kind, ORIGIN), ("other", span, kind, ORIGIN)})
            offer(span, kind, ORIGIN)
            for dx in (1, 3) if KINDS[span][kind][1] else ():
                arrivals.append((SPECIAL_AT[span], "wait", span, kind, (0, dx, 0)))
    pump()
    total = 2 * 2 * 2 * 32
    while True:
        arrivals.sort()
        while arrivals and arrivals[0][0] <= state["now"]:
            land(arrivals.pop(0))
            arrivals.sort()
        pump()
        due_tasks.sort()
        now = state["now"]
        ready = None
        for name in ORDER:
            if now < WORK_AT[name[0] == "w"] or not todo[name]:
                continue
            options = [p for p in todo[name] if name != "hg1" or p in done["hg0"]]
            if name[0] == "w":
                options = [p for p in options if p in done["h" + name[1:]]]
            if options:
                ready = (name, options[0])
                break
        if due_tasks and due_tasks[0][0] <= now and not (due_tasks[0][1] == "blend" and not done["wg0"]):
            name = due_tasks.pop(0)[1]
            steps.append(("task", name) + ((len(done["wg1"]) > 0,) if name == "blend" else ()))
            flags.add(name)
            state["now"] += 1.5
            if name in ("reduce", "outer"):
                free_at[3] = max(state["now"], free_at[3]) + per_kib * island_kib
                queued[3].append(free_at[3])
                due_tasks.append((free_at[3] + LATENCY[3], "outer" if name == "reduce" else "relay"))
            elif name == "relay":
                due_tasks.append((state["now"] + 8.0, "lend"))
            elif name == "lend":
                due_tasks.append((max(state["now"] + 26.0, WORK_AT[1] + 4.0), "blend"))
        elif len(done["wg0"]) == len(PAIRS) and "blend" in flags and "end0" not in flags:
            steps.append(("task", "end0"))
            flags.add("end0")
            state["now"] += 2.0
        elif ready:
            name, pair = ready
            took = options[:2] if name[0] == "w" else pair
            steps.append(("task", name[:2], int(name[2]), took, not done[name] and not (name == "wg1" and "blend" in flags)))
            for one in took if name[0] == "w" else [pair]:
                todo[name].remove(one)
                done[name].add(one)
                state["now"] += TASK_TIMES[int(name[2])][name[0] == "w"]
        elif len(have) == total and len(done["wg1"]) == len(PAIRS) and not due_tasks:
            break
        else:
            times = [t[0] for t in arrivals[:1]] + [t[0] for t in due_tasks]
            for link, q in enumerate(queued):
                if len(q) >= DEPTH and heaps[link]:
                    times.append(min(q))
            times = [t for t in times if t > now]
            state["now"] = min(times) if times else now + 0.1
            if len(have) == total and len(done["wg1"]) == len(PAIRS):
                break
    while due_tasks:
        steps.append(("task", due_tasks.pop(0)[1]))
    last = max(i for i, s in enumerate(steps) if s[0] == "task" and s[1] == "wg")
    steps[last] = ("task", "end1", steps[last][3])
    return steps, sent_rows, state["now"], finished


def kernel(
    hidden, cotangent, local_weight, pending, global_weight, outer_momentum,
    hidden_grad, merged, new_global, new_momentum, fresh, lent,
    c_lo, c_hi, h_buf, w_buf, acc, part, p_buf, pc_buf, py_buf, g_buf, m_buf,
    send_sem, mine_sem, across_sem, other_sem, seed_sem, special_sem, swap_send, swap_recv,
    load_sem, hg_sem, hg_send, hg_recv, out_sem, back_send, back_recv, isl_send, isl_recv,
):
    island = lax.axis_index("island")
    mp = lax.axis_index("mp")
    z, x, yh = mp // 8, (mp // 2) % 4, mp % 2
    core, yl = island % 2, island // 2
    role = lax.rem(core + x, 2)
    c_bufs = (c_lo, c_hi)

    def mp_at(pz, px, py):
        return (lax.rem(pz, 4) * 4 + lax.rem(px, 4)) * 2 + lax.rem(py, 2)

    partner = [
        {"mp": mp_at(z + 1, x, yh)},
        {"mp": mp_at(z + 3, x, yh)},
        {"mp": mp_at(z, x + 2, yh)},
        {"mp": mp_at(z, x, yh + 1)},
    ]
    other_core = {"island": yl * 2 + 1 - core}
    other_y = {"island": (1 - yl) * 2 + core}

    def beside(step, its_role):
        return {"island": yl * 2 + lax.rem(x + 1 + its_role, 2), "mp": mp_at(z, x + step, yh)}

    def only(which, action):
        pl.when(role == which)(action)

    def remote(src, dst, ssem, rsem, device):
        return pltpu.make_async_remote_copy(src, dst, ssem, rsem, device_id=device, device_id_type=MESH)

    def quarter(ref, index):
        return ref.at[:, pl.ds(pl.multiple_of(index * 1024, 1024), 1024)]

    def half(index):
        return pl.ds(index * HALF, HALF)

    own = [
        pltpu.make_async_copy(
            cotangent.at[:, pl.ds(*SPANS[span])],
            c_bufs[span].at[pl.ds(pl.multiple_of(mp * SHARD, SHARD), SHARD)],
            load_sem.at[span],
        )
        for span in (0, 1)
    ]
    w_load = pltpu.make_async_copy(local_weight, w_buf, load_sem.at[2])
    h_load = pltpu.make_async_copy(hidden, h_buf, load_sem.at[3])
    g_load = pltpu.make_async_copy(global_weight, g_buf, load_sem.at[4])
    m_load = pltpu.make_async_copy(outer_momentum, m_buf, load_sem.at[5])
    mine, theirs = yl * 2 + core, (1 - yl) * 2 + core
    p_loads = [
        pltpu.make_async_copy(quarter(pending, theirs), p_buf.at[0], load_sem.at[6]),
        pltpu.make_async_copy(quarter(pending, mine), p_buf.at[1], load_sem.at[7]),
    ]

    @pl.when(role == 0)
    def _():
        for copy in own + [w_load, h_load]:
            copy.start()

    for copy in p_loads + [g_load, m_load]:
        copy.start()

    barrier = pltpu.get_barrier_semaphore()
    greeted = partner + [other_core, other_y] + [beside(step, r) for step in (1, 3) for r in (0, 1)]
    for device in greeted:
        pl.semaphore_signal(barrier, inc=1, device_id=device, device_id_type=MESH)
    pl.semaphore_wait(barrier, len(greeted))

    def index_of(offset):
        return (offset[0] * 4 + offset[1]) * 2 + offset[2]

    def rows_of(offset):
        dz, dx, dy = offset
        return mp_at(z + 4 - dz, x + 4 - dx, yh + dy) * SHARD

    def place(span, kind, offset, side):
        first, rows = KINDS[span][kind]
        return c_bufs[span].at[pl.ds(pl.multiple_of(rows_of(offset) + side * 64 + first, 16), rows)]

    def place_all(span, offset, side):
        return c_bufs[span].at[pl.ds(pl.multiple_of(rows_of(offset) + side * 64, 16), 64)]

    def send(span, kind, offset, link):
        ref = place(span, kind, offset, role)
        remote(
            ref, ref, send_sem.at[link, span], mine_sem.at[span, kind, index_of(moved(offset, link))], partner[link]
        ).start()

    def wait(span, kind, offset):
        ref = place(span, kind, offset, role)
        remote(ref, ref, send_sem.at[0, span], mine_sem.at[span, kind, index_of(offset)], partner[0]).wait_recv()

    def across(span, offset):
        ref = place_all(span, offset, role)
        remote(ref, ref, across_sem.at[span], other_sem.at[span, index_of(offset)], other_core).start()

    def other(span, offset):
        ref = place_all(span, offset, 1 - role)
        remote(ref, ref, across_sem.at[span], other_sem.at[span, index_of(offset)], other_core).wait_recv()

    def seed_copy(span):
        ref = c_bufs[span].at[pl.ds(pl.multiple_of(mp * SHARD, SHARD), SHARD)]
        return remote(ref, ref, seed_sem.at[0, span], seed_sem.at[1, span], other_core)

    def specials(span):
        for kind in (0, 1):
            first, rows = KINDS[span][kind]
            if not rows:
                continue
            for side in (0, 1):
                src = cotangent.at[pl.ds(side * 64 + first, rows), pl.ds(*SPANS[span])]
                dst = place(span, kind, ORIGIN, side)
                for step in (1, 3):
                    remote(
                        src, dst, special_sem.at[span], mine_sem.at[span, kind, index_of((0, step, 0))], beside(step, side)
                    ).start()

    def seed(span):
        @pl.when(role == 0)
        def _():
            own[span].wait()
            seed_copy(span).start()

        @pl.when(role == 1)
        def _():
            specials(span)
            seed_copy(span).wait_recv()

    swaps = [
        remote(source.at[half(i)], target.at[half(i)], swap_send.at[j, i], swap_recv.at[j, i], beside((1, 3)[i], 1))
        for j, (source, target) in enumerate(((local_weight, w_buf), (hidden, h_buf)))
        for i in (0, 1)
    ]

    def swap(which):
        @pl.when(role == 1)
        def _():
            for copy in swaps[2 * which : 2 * which + 2]:
                copy.start()

    pair_sum = [
        remote(quarter(pending, i * 2 + 1 - core), pc_buf.at[i], isl_send.at[i], isl_recv.at[i], other_core) for i in (0, 1)
    ]
    for copy in pair_sum:
        copy.start()
    to_y = remote(p_buf.at[0], py_buf, isl_send.at[2], isl_recv.at[2], other_y)
    fresh_y = remote(p_buf.at[1], quarter(fresh, mine), isl_send.at[3], isl_recv.at[3], other_y)
    fresh_c = remote(p_buf.at[1], quarter(fresh, mine), isl_send.at[4], isl_recv.at[4], other_core)
    relay_c = remote(quarter(fresh, theirs), quarter(fresh, theirs), isl_send.at[5], isl_recv.at[5], other_core)
    fresh_own = pltpu.make_async_copy(p_buf.at[1], quarter(fresh, mine), out_sem.at[4])
    ng_out = pltpu.make_async_copy(g_buf, new_global, out_sem.at[0])
    nm_out = pltpu.make_async_copy(m_buf, new_momentum, out_sem.at[1])

    backward_scale = 1.0 / math.sqrt(D)
    blend = -mix_weight * inner_rate / math.sqrt(TOKENS)
    tile = 64

    def by_tile(step):
        def one(i, _):
            step(pl.ds(pl.multiple_of(i * tile, tile), tile))
            return 0

        lax.fori_loop(0, FF_SHARE // tile, one, 0)

    def wide(value):
        return value.astype(jnp.float32)

    def reduce():
        for copy in p_loads + pair_sum:
            copy.wait()

        def step(rows):
            p_buf[0, rows] = (wide(p_buf[0, rows]) + wide(pc_buf[1 - yl, rows])).astype(jnp.bfloat16)

        by_tile(step)
        to_y.start()

    def outer():
        g_load.wait()
        m_load.wait()
        to_y.wait()

        def step(rows):
            mean = (wide(p_buf[1, rows]) + wide(pc_buf[yl, rows]) + wide(py_buf[rows])) / islands
            momentum = decay_rate * m_buf[rows] + mean
            weight = g_buf[rows] - outer_rate * (mean + decay_rate * momentum)
            m_buf[rows] = momentum
            g_buf[rows] = weight
            p_buf[1, rows] = weight.astype(jnp.bfloat16)

        by_tile(step)
        for copy in (fresh_y, fresh_c, fresh_own, ng_out, nm_out):
            copy.start()

    def relay():
        fresh_y.wait()
        relay_c.start()

    lends = [remote(fresh.at[half(i)], lent.at[half(i)], back_send.at[2, i], back_recv.at[2, i], beside((1, 3)[i], 1)) for i in (0, 1)]

    def lend():
        fresh_c.wait()
        fresh_own.wait()
        relay_c.wait()

        @pl.when(role == 1)
        def _():
            for copy in lends:
                copy.start()

    def fresh_load(source, index, slot):
        return pltpu.make_async_copy(quarter(source, index), p_buf.at[slot], load_sem.at[8 + slot])

    def start_fresh(index, slot):
        only(0, fresh_load(fresh, index, slot).start)
        only(1, fresh_load(lent, index, slot).start)

    def blend_all(started):
        @pl.when(role == 1)
        def _():
            for copy in lends:
                copy.wait()

        start_fresh(0, 0)
        for index in range(4):
            slot = index % 2
            fresh_load(fresh, index, slot).wait()
            if index < 3:
                start_fresh(index + 1, 1 - slot)

            def step(rows, slot=slot, index=index):
                for side in (0, 1):
                    first = index * 1024 + side * 512
                    columns = pl.ds(first, 512)
                    base = mix_weight * wide(w_buf[rows, columns]) + (1.0 - mix_weight) * wide(
                        p_buf[slot, rows, pl.ds(side * 512, 512)]
                    )
                    base = base * (1.0 / blend)
                    if first < CUT or started:
                        base = base + acc[rows, columns]
                    acc[rows, columns] = base

            by_tile(step)

    def pair_tokens(pair):
        return pl.ds(pl.multiple_of(mp_at(z + 4 - pair[0], x + 4 - pair[1], 0) * SHARD, 2 * SHARD), 2 * SHARD)

    def hg_out(tokens):
        return pltpu.make_async_copy(part.at[:, tokens], hidden_grad.at[:, tokens], hg_sem.at[0])

    def hg_back(i, tokens):
        return remote(
            part.at[half(i), tokens], hidden_grad.at[half(i), tokens], hg_send.at[i], hg_recv.at[i], beside((3, 1)[i], 1)
        )

    def hg(span, pair, start):
        tokens = pair_tokens(pair)
        if span == 0 and start:
            only(0, w_load.wait)

            @pl.when(role == 1)
            def _():
                for copy in swaps[:2]:
                    copy.wait()

        first, columns = SPANS[span]
        block = lax.dot_general(
            w_buf[:, pl.ds(first, columns)],
            c_bufs[span][tokens],
            (((1,), (1,)), ((), ())),
            preferred_element_type=jnp.float32,
        )
        if span == 0:
            part[:, tokens] = (block * backward_scale).astype(jnp.bfloat16)
            return
        part[:, tokens] = (wide(part[:, tokens]) + block * backward_scale).astype(jnp.bfloat16)

        @pl.when(role == 0)
        def _():
            hg_out(tokens).start()

        @pl.when(role == 1)
        def _():
            for i in (0, 1):
                hg_back(i, tokens).start()

    width = 512

    def product(span, pairs, i):
        columns = pl.ds(pl.multiple_of(i * width, width), width)
        there = pl.ds(pl.multiple_of(SPANS[span][0] + i * width, width), width)
        total = None
        for pair in pairs:
            tokens = pair_tokens(pair)
            block = jnp.dot(h_buf[:, tokens], c_bufs[span][tokens, columns], preferred_element_type=jnp.float32)
            total = block if total is None else total + block
        return there, total

    def wg(span, pairs, start):
        if span == 0 and start:
            only(0, h_load.wait)

            @pl.when(role == 1)
            def _():
                for copy in swaps[2:]:
                    copy.wait()

        def step(i, _):
            there, total = product(span, pairs, i)
            acc[:, there] = total if start else acc[:, there] + total
            return 0

        lax.fori_loop(0, SPANS[span][1] // width, step, 0)

    lo, hi = pl.ds(0, CUT), pl.ds(CUT, D - CUT)
    out_lo = pltpu.make_async_copy(w_buf.at[:, lo], merged.at[:, lo], out_sem.at[2])
    out_hi = pltpu.make_async_copy(w_buf.at[:, hi], merged.at[:, hi], out_sem.at[3])
    def backs(span, j):
        return [
            remote(
                w_buf.at[half(i), span], merged.at[half(i), span], back_send.at[j, i], back_recv.at[j, i], beside((3, 1)[i], 1)
            )
            for i in (0, 1)
        ]

    back_lo = backs(lo, 0)
    back_hi = [backs(pl.ds(first, width), 3 + j) for j, first in enumerate(range(CUT, D, width))]

    def end0():
        def step(i, _):
            columns = pl.ds(pl.multiple_of(i * width, width), width)
            w_buf[:, columns] = (acc[:, columns] * blend).astype(jnp.bfloat16)
            return 0

        lax.fori_loop(0, CUT // width, step, 0)
        only(0, out_lo.start)

        @pl.when(role == 1)
        def _():
            for copy in back_lo:
                copy.start()

    def end1(pairs):
        for i in range((D - CUT) // width):
            there, total = product(1, pairs, i)
            w_buf[:, there] = ((acc[:, there] + total) * blend).astype(jnp.bfloat16)

            @pl.when(role == 1)
            def _(i=i):
                for copy in back_hi[i]:
                    copy.start()

        only(0, out_hi.start)

    def finish1():
        @pl.when(role == 0)
        def _():
            out_lo.wait()
            out_hi.wait()
            hg_out(pl.ds(0, TOKENS)).wait()

        @pl.when(role == 1)
        def _():
            for copy in sum(back_hi, back_lo):
                copy.wait()
            for i in (0, 1):
                hg_back(i, pl.ds(0, TOKENS)).wait()

    tasks = {
        "swap_w": lambda: swap(0), "swap_h": lambda: swap(1), "reduce": reduce, "outer": outer, "relay": relay, "lend": lend, "blend": blend_all,
        "hg": hg, "wg": wg, "end0": end0, "end1": end1,
    }
    moves = {"seed": seed, "send": send, "wait": wait, "across": across, "other": other}
    steps, sent_rows = plan()[:2]
    for step in steps:
        if step[0] == "task":
            tasks[step[1]](*step[2:])
        else:
            if step[0] == "other" and step[2] == ORIGIN:
                continue
            moves[step[0]](*step[1:])
    finish1()
    ng_out.wait()
    nm_out.wait()
    for span in (0, 1):
        for link in range(len(LINKS)):
            whole = c_bufs[span].at[pl.ds(0, sent_rows[link][span])]
            remote(whole, whole, send_sem.at[link, span], mine_sem.at[0, 0, 0], partner[link]).wait_send()
        whole = c_bufs[span].at[pl.ds(0, 31 * 64)]
        remote(whole, whole, across_sem.at[span], other_sem.at[span, 0], other_core).wait_send()
        only(0, seed_copy(span).wait_send)

        @pl.when(role == 1)
        def _():
            whole = c_bufs[span].at[pl.ds(0, 2 * SHARD)]
            remote(whole, whole, special_sem.at[span], mine_sem.at[0, 0, 0], beside(1, 1)).wait_send()


def hand_on(*refs):
    sources, targets, bufs, sems = refs[:4], refs[4:8], refs[8:12], refs[12]
    ins, outs = [], []
    for source, target, buf in zip(sources, targets, bufs):
        rows = source.shape[0] // SPLIT
        for i in range(SPLIT):
            part = pl.ds(i * rows, rows)
            ins.append(pltpu.make_async_copy(source.at[part], buf.at[part], sems.at[len(ins)]))
            outs.append(pltpu.make_async_copy(buf.at[part], target.at[part], sems.at[len(outs) + 4 * SPLIT]))
    for copy in ins:
        copy.start()
    for copy, out in zip(ins, outs):
        copy.wait()
        out.start()
    for out in outs:
        out.wait()


SPLIT = 4


def body(hidden, cotangent, local_weight, pending, global_weight, outer_momentum):
    big = jax.ShapeDtypeStruct((FF_SHARE, D), jnp.bfloat16)
    state = jax.ShapeDtypeStruct((FF_SHARE, D // islands), jnp.float32)
    dma = pltpu.SemaphoreType.DMA
    outs = pl.pallas_call(
        kernel,
        out_shape=(big, big, state, state, big, big),
        in_specs=[pl.BlockSpec(memory_space=pl.ANY)] * 6,
        out_specs=[pl.BlockSpec(memory_space=pl.ANY)] * 6,
        scratch_shapes=[
            pltpu.VMEM((TOKENS, CUT), jnp.bfloat16),
            pltpu.VMEM((TOKENS, D - CUT), jnp.bfloat16),
            pltpu.VMEM((FF_SHARE, TOKENS), jnp.bfloat16),
            pltpu.VMEM((FF_SHARE, D), jnp.bfloat16),
            pltpu.VMEM((FF_SHARE, D), jnp.float32),
            pltpu.VMEM((FF_SHARE, TOKENS), jnp.bfloat16),
            pltpu.VMEM((2, FF_SHARE, 1024), jnp.bfloat16),
            pltpu.VMEM((2, FF_SHARE, 1024), jnp.bfloat16),
            pltpu.VMEM((FF_SHARE, 1024), jnp.bfloat16),
            pltpu.VMEM((FF_SHARE, 1024), jnp.float32),
            pltpu.VMEM((FF_SHARE, 1024), jnp.float32),
            dma((len(LINKS), 2)),
            dma((2, 2, 32)),
            dma((2,)),
            dma((2, 32)),
            dma((2, 2)),
            dma((2,)),
            dma((2, 2)),
            dma((2, 2)),
            dma((14,)),
            dma((1,)),
            dma((2,)),
            dma((2,)),
            dma((5,)),
            dma((7, 2)),
            dma((7, 2)),
            dma((6,)),
            dma((6,)),
        ],
        compiler_params=pltpu.CompilerParams(collective_id=0, has_side_effects=True, vmem_limit_bytes=63 * MIB),
        cost_estimate=pl.CostEstimate(flops=4 * TOKENS * D * FF_SHARE, bytes_accessed=64 * MIB, transcendentals=0),
        name="gather_and_update",
    )(hidden[0].T, cotangent[0], local_weight[0].T, pending[0].T, global_weight.T, outer_momentum.T)
    outs = pl.pallas_call(
        hand_on,
        out_shape=(big, big, state, state),
        in_specs=[pl.BlockSpec(memory_space=pl.ANY)] * 4,
        out_specs=[pl.BlockSpec(memory_space=pl.ANY)] * 4,
        scratch_shapes=[pltpu.VMEM((FF_SHARE, D), jnp.bfloat16)] * 2 + [pltpu.VMEM((FF_SHARE, 1024), jnp.float32)] * 2 + [pltpu.SemaphoreType.DMA((8 * SPLIT,))],
        compiler_params=pltpu.CompilerParams(vmem_limit_bytes=60 * MIB),
        name="hand_on",
    )(*outs[:4])
    return outs[0].T[None], outs[1].T[None], outs[2].T, outs[3].T


def solution(mesh):
    placed = (
        P("island", None, "mp"),
        P("island", "mp", None),
        P("island", None, "mp"),
        P("island", None, "mp"),
        P("island", "mp"),
        P("island", "mp"),
    )
    return jax.shard_map(
        body,
        mesh=mesh,
        in_specs=placed,
        out_specs=(
            P("island", None, "mp"),
            P("island", None, "mp"),
            P("island", "mp"),
            P("island", "mp"),
        ),
        check_vma=False,
    )
```

```python
import math

import jax
import jax.numpy as jnp
from jax import lax
from jax.experimental import pallas as pl
from jax.experimental.pallas import tpu as pltpu
from jax.sharding import PartitionSpec as P

D = 4096
TOKENS = 4096
FF_SHARE = 448
SHARD = 128
HALF = FF_SHARE // 2
CUT = 2048

inner_rate = 0.3
outer_rate = 0.7
decay_rate = 0.9
mix_weight = 0.5
islands = 4

MESH = pl.DeviceIdType.MESH
MIB = 2**20

KINDS = (((0, 64), (0, 0)), ((0, 32), (32, 32)))
SPANS = ((0, CUT), (CUT, D - CUT))
LINKS = ((0, 1), (0, -1), (1, 2), (2, 1))
WRAP = (4, 4, 2)
ORIGIN = (0, 0, 0)
OFFSETS = tuple((dz, dx, dy) for dz in range(4) for dx in range(4) for dy in range(2))


def moved(offset, link):
    axis, step = LINKS[link]
    out = list(offset)
    out[axis] = (out[axis] + step) % WRAP[axis]
    return tuple(out)


def links_of(kind, offset):
    dz, dx, dy = offset
    found = []
    if offset == ORIGIN:
        found.append(2)
    if kind == 0 and dz == 0 and dy == 0:
        found.append(3)
    if kind == 1 and dy == 0:
        found.append(3)
    if kind == 0 or dy == 0:
        way = 1 if (dx + dy) % 2 == 0 else -1
        if dz == 0 or (dz == 1 and way == 1):
            found.append(0)
        if dz == 0 or (dz == 3 and way == -1):
            found.append(1)
    return found


def order_of(pair):
    dz, dx = min(pair[0], 4 - pair[0]), min(pair[1], 4 - pair[1])
    return (dz, dx, pair)


PAIRS = sorted(((dz, dx) for dz in range(4) for dx in range(4)), key=order_of)
DUE = ((24.0, 65.8), (59.8, 72.9))
HOP = 3.0
ORDER = ("hg0", "wg0", "hg1", "wg1")
TASK_TIMES = ((1.0, 0.83), (1.15, 0.83))
DEPTH = 2
LATENCY = (3.0, 3.0, 4.0, 5.0)
ISLAND_AT = 7.0
SWAP_AT = (18.0, 36.0)
WORK_AT = (46.0, 64.0)
SPECIAL_AT = (16.0, 23.0)


def due_of(span, kind, offset):
    first, last = DUE[span]
    best = first + (last - first) * PAIRS.index(offset[:2]) / (len(PAIRS) - 1)
    for link in links_of(kind, offset):
        best = min(best, due_of(span, kind, moved(offset, link)) - HOP)
    return best


def plan():
    per_kib = 22.4 / 1024
    heaps = [[] for _ in LINKS]
    free_at = [0.0, 0.0, 8.0, 0.0]
    queued = [[] for _ in LINKS]
    arrivals = []
    steps = []
    have = set()
    sent_rows = [[0, 0] for _ in LINKS]
    state = {"now": 0.0}
    todo = {"hg0": [], "wg0": [], "hg1": [], "wg1": []}
    done = {"hg0": set(), "wg0": set(), "hg1": set(), "wg1": set()}
    flags = set()
    due_tasks = [(SWAP_AT[0], "swap_w"), (SWAP_AT[1], "swap_h"), (ISLAND_AT, "reduce")]
    island_kib = FF_SHARE * 2
    finished = []

    def offer(span, kind, offset):
        for link in links_of(kind, offset) if KINDS[span][kind][1] else ():
            heaps[link].append((due_of(span, kind, moved(offset, link)), span, kind, offset))

    def pump():
        now = state["now"]
        for link in range(len(LINKS)):
            while True:
                queued[link] = [t for t in queued[link] if t > now]
                if len(queued[link]) >= DEPTH or not heaps[link]:
                    break
                heaps[link].sort()
                _, span, kind, offset = heaps[link].pop(0)
                rows = KINDS[span][kind][1]
                start = max(now, free_at[link])
                free_at[link] = start + per_kib * rows * SPANS[span][1] / 512
                queued[link].append(free_at[link])
                sent_rows[link][span] += rows
                steps.append(("send", span, kind, offset, link))
                arrivals.append((free_at[link] + LATENCY[link], "wait", span, kind, moved(offset, link)))

    def check(span, offset):
        pair = offset[:2]
        if all((w, span, k, pair + (dy,)) in have for w in ("wait", "other") for k in (0, 1) for dy in (0, 1)):
            todo[f"hg{span}"].append(pair)
            todo[f"wg{span}"].append(pair)
            finished.append((round(state["now"], 1), span, pair))

    def land(entry):
        _, what, span, kind, offset = entry
        state["now"] += 0.06
        if what == "other":
            steps.append(("other", span, offset))
            have.update({("other", span, 0, offset), ("other", span, 1, offset)})
        else:
            steps.append(("wait", span, kind, offset))
            have.add(("wait", span, kind, offset))
            if not KINDS[span][1 - kind][1]:
                have.add(("wait", span, 1 - kind, offset))
            offer(span, kind, offset)
            if ("wait", span, 1 - kind, offset) in have:
                steps.append(("across", span, offset))
                arrivals.append((state["now"] + 4.0, "other", span, 0, offset))
        check(span, offset)

    for span in (0, 1):
        steps.append(("seed", span))
        for kind in (0, 1):
            have.update({("wait", span, kind, ORIGIN), ("other", span, kind, ORIGIN)})
            offer(span, kind, ORIGIN)
            for dx in (1, 3) if KINDS[span][kind][1] else ():
                arrivals.append((SPECIAL_AT[span], "wait", span, kind, (0, dx, 0)))
    pump()
    total = 2 * 2 * 2 * 32
    while True:
        arrivals.sort()
        while arrivals and arrivals[0][0] <= state["now"]:
            land(arrivals.pop(0))
            arrivals.sort()
        pump()
        due_tasks.sort()
        now = state["now"]
        ready = None
        for name in ORDER:
            if now < WORK_AT[name[0] == "w"] or not todo[name]:
                continue
            options = [p for p in todo[name] if name != "hg1" or p in done["hg0"]]
            if name[0] == "w":
                options = [p for p in options if p in done["h" + name[1:]]]
            if options:
                ready = (name, options[0])
                break
        if due_tasks and due_tasks[0][0] <= now and not (due_tasks[0][1] == "blend" and not done["wg0"]):
            name = due_tasks.pop(0)[1]
            steps.append(("task", name) + ((len(done["wg1"]) > 0,) if name == "blend" else ()))
            flags.add(name)
            state["now"] += 1.5
            if name in ("reduce", "outer"):
                free_at[3] = max(state["now"], free_at[3]) + per_kib * island_kib
                queued[3].append(free_at[3])
                due_tasks.append((free_at[3] + LATENCY[3], "outer" if name == "reduce" else "relay"))
            elif name == "relay":
                due_tasks.append((state["now"] + 8.0, "lend"))
            elif name == "lend":
                due_tasks.append((max(state["now"] + 26.0, WORK_AT[1] + 4.0), "blend"))
        elif len(done["wg0"]) == len(PAIRS) and "blend" in flags and "end0" not in flags:
            steps.append(("task", "end0"))
            flags.add("end0")
            state["now"] += 2.0
        elif ready:
            name, pair = ready
            took = options[:2] if name[0] == "w" else pair
            steps.append(("task", name[:2], int(name[2]), took, not done[name] and not (name == "wg1" and "blend" in flags)))
            for one in took if name[0] == "w" else [pair]:
                todo[name].remove(one)
                done[name].add(one)
                state["now"] += TASK_TIMES[int(name[2])][name[0] == "w"]
        elif len(have) == total and len(done["wg1"]) == len(PAIRS) and not due_tasks:
            break
        else:
            times = [t[0] for t in arrivals[:1]] + [t[0] for t in due_tasks]
            for link, q in enumerate(queued):
                if len(q) >= DEPTH and heaps[link]:
                    times.append(min(q))
            times = [t for t in times if t > now]
            state["now"] = min(times) if times else now + 0.1
            if len(have) == total and len(done["wg1"]) == len(PAIRS):
                break
    while due_tasks:
        steps.append(("task", due_tasks.pop(0)[1]))
    last = max(i for i, s in enumerate(steps) if s[0] == "task" and s[1] == "wg")
    steps[last] = ("task", "end1", steps[last][3])
    return steps, sent_rows, state["now"], finished


def kernel(
    hidden, cotangent, local_weight, pending, global_weight, outer_momentum,
    hidden_grad, merged, new_global, new_momentum, fresh, lent,
    c_lo, c_hi, h_buf, w_buf, acc, part, p_buf, pc_buf, py_buf, g_buf, m_buf,
    send_sem, mine_sem, across_sem, other_sem, seed_sem, special_sem, swap_send, swap_recv,
    load_sem, hg_sem, hg_send, hg_recv, out_sem, back_send, back_recv, isl_send, isl_recv,
):
    island = lax.axis_index("island")
    mp = lax.axis_index("mp")
    z, x, yh = mp // 8, (mp // 2) % 4, mp % 2
    core, yl = island % 2, island // 2
    role = lax.rem(core + x, 2)
    c_bufs = (c_lo, c_hi)

    def mp_at(pz, px, py):
        return (lax.rem(pz, 4) * 4 + lax.rem(px, 4)) * 2 + lax.rem(py, 2)

    partner = [
        {"mp": mp_at(z + 1, x, yh)},
        {"mp": mp_at(z + 3, x, yh)},
        {"mp": mp_at(z, x + 2, yh)},
        {"mp": mp_at(z, x, yh + 1)},
    ]
    other_core = {"island": yl * 2 + 1 - core}
    other_y = {"island": (1 - yl) * 2 + core}

    def beside(step, its_role):
        return {"island": yl * 2 + lax.rem(x + 1 + its_role, 2), "mp": mp_at(z, x + step, yh)}

    def only(which, action):
        pl.when(role == which)(action)

    def remote(src, dst, ssem, rsem, device):
        return pltpu.make_async_remote_copy(src, dst, ssem, rsem, device_id=device, device_id_type=MESH)

    def quarter(ref, index):
        return ref.at[:, pl.ds(pl.multiple_of(index * 1024, 1024), 1024)]

    def half(index):
        return pl.ds(index * HALF, HALF)

    own = [
        pltpu.make_async_copy(
            cotangent.at[:, pl.ds(*SPANS[span])],
            c_bufs[span].at[pl.ds(pl.multiple_of(mp * SHARD, SHARD), SHARD)],
            load_sem.at[span],
        )
        for span in (0, 1)
    ]
    w_load = pltpu.make_async_copy(local_weight, w_buf, load_sem.at[2])
    h_load = pltpu.make_async_copy(hidden, h_buf, load_sem.at[3])
    g_load = pltpu.make_async_copy(global_weight, g_buf, load_sem.at[4])
    m_load = pltpu.make_async_copy(outer_momentum, m_buf, load_sem.at[5])
    mine, theirs = yl * 2 + core, (1 - yl) * 2 + core
    p_loads = [
        pltpu.make_async_copy(quarter(pending, theirs), p_buf.at[0], load_sem.at[6]),
        pltpu.make_async_copy(quarter(pending, mine), p_buf.at[1], load_sem.at[7]),
    ]

    @pl.when(role == 0)
    def _():
        for copy in own + [w_load, h_load]:
            copy.start()

    for copy in p_loads + [g_load, m_load]:
        copy.start()

    barrier = pltpu.get_barrier_semaphore()
    greeted = partner + [other_core, other_y] + [beside(step, r) for step in (1, 3) for r in (0, 1)]
    for device in greeted:
        pl.semaphore_signal(barrier, inc=1, device_id=device, device_id_type=MESH)
    pl.semaphore_wait(barrier, len(greeted))

    def index_of(offset):
        return (offset[0] * 4 + offset[1]) * 2 + offset[2]

    def rows_of(offset):
        dz, dx, dy = offset
        return mp_at(z + 4 - dz, x + 4 - dx, yh + dy) * SHARD

    def place(span, kind, offset, side):
        first, rows = KINDS[span][kind]
        return c_bufs[span].at[pl.ds(pl.multiple_of(rows_of(offset) + side * 64 + first, 16), rows)]

    def place_all(span, offset, side):
        return c_bufs[span].at[pl.ds(pl.multiple_of(rows_of(offset) + side * 64, 16), 64)]

    def send(span, kind, offset, link):
        ref = place(span, kind, offset, role)
        remote(
            ref, ref, send_sem.at[link, span], mine_sem.at[span, kind, index_of(moved(offset, link))], partner[link]
        ).start()

    def wait(span, kind, offset):
        ref = place(span, kind, offset, role)
        remote(ref, ref, send_sem.at[0, span], mine_sem.at[span, kind, index_of(offset)], partner[0]).wait_recv()

    def across(span, offset):
        ref = place_all(span, offset, role)
        remote(ref, ref, across_sem.at[span], other_sem.at[span, index_of(offset)], other_core).start()

    def other(span, offset):
        ref = place_all(span, offset, 1 - role)
        remote(ref, ref, across_sem.at[span], other_sem.at[span, index_of(offset)], other_core).wait_recv()

    def seed_copy(span):
        ref = c_bufs[span].at[pl.ds(pl.multiple_of(mp * SHARD, SHARD), SHARD)]
        return remote(ref, ref, seed_sem.at[0, span], seed_sem.at[1, span], other_core)

    def specials(span):
        for kind in (0, 1):
            first, rows = KINDS[span][kind]
            if not rows:
                continue
            for side in (0, 1):
                src = cotangent.at[pl.ds(side * 64 + first, rows), pl.ds(*SPANS[span])]
                dst = place(span, kind, ORIGIN, side)
                for step in (1, 3):
                    remote(
                        src, dst, special_sem.at[span], mine_sem.at[span, kind, index_of((0, step, 0))], beside(step, side)
                    ).start()

    def seed(span):
        @pl.when(role == 0)
        def _():
            own[span].wait()
            seed_copy(span).start()

        @pl.when(role == 1)
        def _():
            specials(span)
            seed_copy(span).wait_recv()

    swaps = [
        remote(source.at[half(i)], target.at[half(i)], swap_send.at[j, i], swap_recv.at[j, i], beside((1, 3)[i], 1))
        for j, (source, target) in enumerate(((local_weight, w_buf), (hidden, h_buf)))
        for i in (0, 1)
    ]

    def swap(which):
        @pl.when(role == 1)
        def _():
            for copy in swaps[2 * which : 2 * which + 2]:
                copy.start()

    pair_sum = [
        remote(quarter(pending, i * 2 + 1 - core), pc_buf.at[i], isl_send.at[i], isl_recv.at[i], other_core) for i in (0, 1)
    ]
    for copy in pair_sum:
        copy.start()
    to_y = remote(p_buf.at[0], py_buf, isl_send.at[2], isl_recv.at[2], other_y)
    fresh_y = remote(p_buf.at[1], quarter(fresh, mine), isl_send.at[3], isl_recv.at[3], other_y)
    fresh_c = remote(p_buf.at[1], quarter(fresh, mine), isl_send.at[4], isl_recv.at[4], other_core)
    relay_c = remote(quarter(fresh, theirs), quarter(fresh, theirs), isl_send.at[5], isl_recv.at[5], other_core)
    fresh_own = pltpu.make_async_copy(p_buf.at[1], quarter(fresh, mine), out_sem.at[4])
    ng_out = pltpu.make_async_copy(g_buf, new_global, out_sem.at[0])
    nm_out = pltpu.make_async_copy(m_buf, new_momentum, out_sem.at[1])

    backward_scale = 1.0 / math.sqrt(D)
    blend = -mix_weight * inner_rate / math.sqrt(TOKENS)
    tile = 64

    def by_tile(step):
        def one(i, _):
            step(pl.ds(pl.multiple_of(i * tile, tile), tile))
            return 0

        lax.fori_loop(0, FF_SHARE // tile, one, 0)

    def wide(value):
        return value.astype(jnp.float32)

    def reduce():
        for copy in p_loads + pair_sum:
            copy.wait()

        def step(rows):
            p_buf[0, rows] = (wide(p_buf[0, rows]) + wide(pc_buf[1 - yl, rows])).astype(jnp.bfloat16)

        by_tile(step)
        to_y.start()

    def outer():
        g_load.wait()
        m_load.wait()
        to_y.wait()

        def step(rows):
            mean = (wide(p_buf[1, rows]) + wide(pc_buf[yl, rows]) + wide(py_buf[rows])) / islands
            momentum = decay_rate * m_buf[rows] + mean
            weight = g_buf[rows] - outer_rate * (mean + decay_rate * momentum)
            m_buf[rows] = momentum
            g_buf[rows] = weight
            p_buf[1, rows] = weight.astype(jnp.bfloat16)

        by_tile(step)
        for copy in (fresh_y, fresh_c, fresh_own, ng_out, nm_out):
            copy.start()

    def relay():
        fresh_y.wait()
        relay_c.start()

    lends = [remote(fresh.at[half(i)], lent.at[half(i)], back_send.at[2, i], back_recv.at[2, i], beside((1, 3)[i], 1)) for i in (0, 1)]

    def lend():
        fresh_c.wait()
        fresh_own.wait()
        relay_c.wait()

        @pl.when(role == 1)
        def _():
            for copy in lends:
                copy.start()

    def fresh_load(source, index, slot):
        return pltpu.make_async_copy(quarter(source, index), p_buf.at[slot], load_sem.at[8 + slot])

    def start_fresh(index, slot):
        only(0, fresh_load(fresh, index, slot).start)
        only(1, fresh_load(lent, index, slot).start)

    def blend_all(started):
        @pl.when(role == 1)
        def _():
            for copy in lends:
                copy.wait()

        start_fresh(0, 0)
        for index in range(4):
            slot = index % 2
            fresh_load(fresh, index, slot).wait()
            if index < 3:
                start_fresh(index + 1, 1 - slot)

            def step(rows, slot=slot, index=index):
                for side in (0, 1):
                    first = index * 1024 + side * 512
                    columns = pl.ds(first, 512)
                    base = mix_weight * wide(w_buf[rows, columns]) + (1.0 - mix_weight) * wide(
                        p_buf[slot, rows, pl.ds(side * 512, 512)]
                    )
                    base = base * (1.0 / blend)
                    if first < CUT or started:
                        base = base + acc[rows, columns]
                    acc[rows, columns] = base

            by_tile(step)

    def pair_tokens(pair):
        return pl.ds(pl.multiple_of(mp_at(z + 4 - pair[0], x + 4 - pair[1], 0) * SHARD, 2 * SHARD), 2 * SHARD)

    def hg_out(tokens):
        return pltpu.make_async_copy(part.at[:, tokens], hidden_grad.at[:, tokens], hg_sem.at[0])

    def hg_back(i, tokens):
        return remote(
            part.at[half(i), tokens], hidden_grad.at[half(i), tokens], hg_send.at[i], hg_recv.at[i], beside((3, 1)[i], 1)
        )

    def hg(span, pair, start):
        tokens = pair_tokens(pair)
        if span == 0 and start:
            only(0, w_load.wait)

            @pl.when(role == 1)
            def _():
                for copy in swaps[:2]:
                    copy.wait()

        first, columns = SPANS[span]
        block = lax.dot_general(
            w_buf[:, pl.ds(first, columns)],
            c_bufs[span][tokens],
            (((1,), (1,)), ((), ())),
            preferred_element_type=jnp.float32,
        )
        if span == 0:
            part[:, tokens] = (block * backward_scale).astype(jnp.bfloat16)
            return
        part[:, tokens] = (wide(part[:, tokens]) + block * backward_scale).astype(jnp.bfloat16)

        @pl.when(role == 0)
        def _():
            hg_out(tokens).start()

        @pl.when(role == 1)
        def _():
            for i in (0, 1):
                hg_back(i, tokens).start()

    width = 512

    def product(span, pairs, i):
        columns = pl.ds(pl.multiple_of(i * width, width), width)
        there = pl.ds(pl.multiple_of(SPANS[span][0] + i * width, width), width)
        total = None
        for pair in pairs:
            tokens = pair_tokens(pair)
            block = jnp.dot(h_buf[:, tokens], c_bufs[span][tokens, columns], preferred_element_type=jnp.float32)
            total = block if total is None else total + block
        return there, total

    def wg(span, pairs, start):
        if span == 0 and start:
            only(0, h_load.wait)

            @pl.when(role == 1)
            def _():
                for copy in swaps[2:]:
                    copy.wait()

        def step(i, _):
            there, total = product(span, pairs, i)
            acc[:, there] = total if start else acc[:, there] + total
            return 0

        lax.fori_loop(0, SPANS[span][1] // width, step, 0)

    lo, hi = pl.ds(0, CUT), pl.ds(CUT, D - CUT)
    out_lo = pltpu.make_async_copy(w_buf.at[:, lo], merged.at[:, lo], out_sem.at[2])
    out_hi = pltpu.make_async_copy(w_buf.at[:, hi], merged.at[:, hi], out_sem.at[3])
    def backs(span, j):
        return [
            remote(
                w_buf.at[half(i), span], merged.at[half(i), span], back_send.at[j, i], back_recv.at[j, i], beside((3, 1)[i], 1)
            )
            for i in (0, 1)
        ]

    back_lo = backs(lo, 0)
    back_hi = [backs(pl.ds(first, width), 3 + j) for j, first in enumerate(range(CUT, D, width))]

    def end0():
        def step(i, _):
            columns = pl.ds(pl.multiple_of(i * width, width), width)
            w_buf[:, columns] = (acc[:, columns] * blend).astype(jnp.bfloat16)
            return 0

        lax.fori_loop(0, CUT // width, step, 0)
        only(0, out_lo.start)

        @pl.when(role == 1)
        def _():
            for copy in back_lo:
                copy.start()

    def end1(pairs):
        for i in range((D - CUT) // width):
            there, total = product(1, pairs, i)
            w_buf[:, there] = ((acc[:, there] + total) * blend).astype(jnp.bfloat16)

            @pl.when(role == 1)
            def _(i=i):
                for copy in back_hi[i]:
                    copy.start()

        only(0, out_hi.start)

    def finish1():
        @pl.when(role == 0)
        def _():
            out_lo.wait()
            out_hi.wait()
            hg_out(pl.ds(0, TOKENS)).wait()

        @pl.when(role == 1)
        def _():
            for copy in sum(back_hi, back_lo):
                copy.wait()
            for i in (0, 1):
                hg_back(i, pl.ds(0, TOKENS)).wait()

    tasks = {
        "swap_w": lambda: swap(0), "swap_h": lambda: swap(1), "reduce": reduce, "outer": outer, "relay": relay, "lend": lend, "blend": blend_all,
        "hg": hg, "wg": wg, "end0": end0, "end1": end1,
    }
    moves = {"seed": seed, "send": send, "wait": wait, "across": across, "other": other}
    steps, sent_rows = plan()[:2]
    for step in steps:
        if step[0] == "task":
            tasks[step[1]](*step[2:])
        else:
            if step[0] == "other" and step[2] == ORIGIN:
                continue
            moves[step[0]](*step[1:])
    finish1()
    ng_out.wait()
    nm_out.wait()
    for span in (0, 1):
        for link in range(len(LINKS)):
            whole = c_bufs[span].at[pl.ds(0, sent_rows[link][span])]
            remote(whole, whole, send_sem.at[link, span], mine_sem.at[0, 0, 0], partner[link]).wait_send()
        whole = c_bufs[span].at[pl.ds(0, 31 * 64)]
        remote(whole, whole, across_sem.at[span], other_sem.at[span, 0], other_core).wait_send()
        only(0, seed_copy(span).wait_send)

        @pl.when(role == 1)
        def _():
            whole = c_bufs[span].at[pl.ds(0, 2 * SHARD)]
            remote(whole, whole, special_sem.at[span], mine_sem.at[0, 0, 0], beside(1, 1)).wait_send()


def hand_on(*refs):
    sources, targets, bufs, sems = refs[:4], refs[4:8], refs[8:12], refs[12]
    ins, outs = [], []
    for source, target, buf in zip(sources, targets, bufs):
        rows = source.shape[0] // SPLIT
        for i in range(SPLIT):
            part = pl.ds(i * rows, rows)
            ins.append(pltpu.make_async_copy(source.at[part], buf.at[part], sems.at[len(ins)]))
            outs.append(pltpu.make_async_copy(buf.at[part], target.at[part], sems.at[len(outs) + 4 * SPLIT]))
    for copy in ins:
        copy.start()
    for copy, out in zip(ins, outs):
        copy.wait()
        out.start()
    for out in outs:
        out.wait()


SPLIT = 4


def body(hidden, cotangent, local_weight, pending, global_weight, outer_momentum):
    big = jax.ShapeDtypeStruct((FF_SHARE, D), jnp.bfloat16)
    state = jax.ShapeDtypeStruct((FF_SHARE, D // islands), jnp.float32)
    dma = pltpu.SemaphoreType.DMA
    outs = pl.pallas_call(
        kernel,
        out_shape=(big, big, state, state, big, big),
        in_specs=[pl.BlockSpec(memory_space=pl.ANY)] * 6,
        out_specs=[pl.BlockSpec(memory_space=pl.ANY)] * 6,
        scratch_shapes=[
            pltpu.VMEM((TOKENS, CUT), jnp.bfloat16),
            pltpu.VMEM((TOKENS, D - CUT), jnp.bfloat16),
            pltpu.VMEM((FF_SHARE, TOKENS), jnp.bfloat16),
            pltpu.VMEM((FF_SHARE, D), jnp.bfloat16),
            pltpu.VMEM((FF_SHARE, D), jnp.float32),
            pltpu.VMEM((FF_SHARE, TOKENS), jnp.bfloat16),
            pltpu.VMEM((2, FF_SHARE, 1024), jnp.bfloat16),
            pltpu.VMEM((2, FF_SHARE, 1024), jnp.bfloat16),
            pltpu.VMEM((FF_SHARE, 1024), jnp.bfloat16),
            pltpu.VMEM((FF_SHARE, 1024), jnp.float32),
            pltpu.VMEM((FF_SHARE, 1024), jnp.float32),
            dma((len(LINKS), 2)),
            dma((2, 2, 32)),
            dma((2,)),
            dma((2, 32)),
            dma((2, 2)),
            dma((2,)),
            dma((2, 2)),
            dma((2, 2)),
            dma((14,)),
            dma((1,)),
            dma((2,)),
            dma((2,)),
            dma((5,)),
            dma((7, 2)),
            dma((7, 2)),
            dma((6,)),
            dma((6,)),
        ],
        compiler_params=pltpu.CompilerParams(collective_id=0, has_side_effects=True, vmem_limit_bytes=63 * MIB),
        cost_estimate=pl.CostEstimate(flops=4 * TOKENS * D * FF_SHARE, bytes_accessed=64 * MIB, transcendentals=0),
        name="gather_and_update",
    )(hidden[0].T, cotangent[0], local_weight[0].T, pending[0].T, global_weight.T, outer_momentum.T)
    outs = pl.pallas_call(
        hand_on,
        out_shape=(big, big, state, state),
        in_specs=[pl.BlockSpec(memory_space=pl.ANY)] * 4,
        out_specs=[pl.BlockSpec(memory_space=pl.ANY)] * 4,
        scratch_shapes=[pltpu.VMEM((FF_SHARE, D), jnp.bfloat16)] * 2 + [pltpu.VMEM((FF_SHARE, 1024), jnp.float32)] * 2 + [pltpu.SemaphoreType.DMA((8 * SPLIT,))],
        compiler_params=pltpu.CompilerParams(vmem_limit_bytes=60 * MIB),
        name="hand_on",
    )(*outs[:4])
    return outs[0].T[None], outs[1].T[None], outs[2].T, outs[3].T


def solution(mesh):
    placed = (
        P("island", None, "mp"),
        P("island", "mp", None),
        P("island", None, "mp"),
        P("island", None, "mp"),
        P("island", "mp"),
        P("island", "mp"),
    )
    return jax.shard_map(
        body,
        mesh=mesh,
        in_specs=placed,
        out_specs=(
            P("island", None, "mp"),
            P("island", None, "mp"),
            P("island", "mp"),
            P("island", "mp"),
        ),
        check_vma=False,
    )
```
